512 devices in a mesh: sec: 16 (over z), gx: 16 (over y_lo, x, core), gy: 2 (over y_hi).
Axes of the slice: x: 4, y: 4 (y_hi: 2, y_lo: 2; y = y_hi * 2 + y_lo), z: 16, core: 2. Of those that a mesh axis runs over, the one named last changes fastest.
Arguments:
- number: float32 [128, 4, 128, 256], P('sec', None, 'gx', 'gy'), may hold values from 0.05 to 1
- cotangent: float32 [128, 4, 128, 256], P('sec', None, 'gx', 'gy'), may hold values from -6 to 6
- growth_rate: float32 [4, 128, 256], P(None, 'gx', 'gy'), may hold values from 1 to 10000
- section_factor: float32 [128], replicated, may hold values from 0.5 to 2
- velocity: float32 [2, 4, 128, 256], P(None, None, 'gx', 'gy'), may hold values from -1 to 1
- diffusivity: float32 [128], replicated, may hold values from 0.05 to 0.4
- kernel: float32 [128, 128], replicated, may hold values from 0.001 to 0.03
- target: int32 [128, 128], replicated, may hold values from 0 to 127, as said below
Outputs:
- number_next: float32 [128, 4, 128, 256], P('sec', None, 'gx', 'gy')
- gradient: float32 [128, 4, 128, 256], P('sec', None, 'gx', 'gy')
The draws below stay inside these ranges and needn't reach their ends.
Inputs may be any that keep to these rules, and one draw needn't show every extreme that they name: target[i, j] is at least the larger of i and j.
All inputs are finite; a program needn't handle non-finite values.
Results may differ from the reference program's by a relative error of at most 0.0001.
Values sent between devices are 32-bit elements; how exact they have to be, the bound alone decides.
No kernel may reach another device: no remote copies, remote signals or barrier semaphores. Data moves between devices by JAX's collectives and lax.ppermute only.
A program may use at most 64 MiB of HBM per device.

```python
import math
import jax
import jax.numpy as jnp
from jax import lax

S = 128
L = 4
NX = 128
NY = 256


def draw_target(key, part):
    rows = lax.broadcasted_iota(jnp.int32, (S, S), 0)
    columns = lax.broadcasted_iota(jnp.int32, (S, S), 1)
    larger = jnp.maximum(rows, columns)
    room = (S - larger).astype(jnp.int32)
    raw_bits = jax.random.randint(key, (S, S), 0, 1 << 20).astype(jnp.int32)
    offsets = (raw_bits % room).astype(jnp.int32)
    return (larger + offsets).astype(jnp.int32)


def block_levels(stream_key, shape, pieces, least, high):
    gain = 1.0
    for axis_at, blocks in pieces:
        draws = jax.random.uniform(jax.random.fold_in(jax.random.fold_in(stream_key, 6), axis_at), (blocks,), jnp.float32, least / len(pieces), high / len(pieces))
        gain = gain * jnp.repeat(jnp.exp(draws), shape[axis_at] // blocks).reshape((-1,) + (1,) * (len(shape) - 1 - axis_at))
    return gain


def gaussian(own_key, extent, deviation, bound, cuts=(), kind=jnp.bfloat16):
    array = jax.random.normal(own_key, extent, jnp.float32) * deviation
    if len(cuts) > 0:
        array = block_levels(own_key, extent, cuts, -0.22, 0.18) * array
    return jnp.clip(array, min=-bound, max=bound).astype(kind)


def setup_inputs(seed: int = 0) -> dict:
    keys = jax.random.split(jax.random.key(seed), 9)
    number = jnp.clip(jnp.exp(math.log(1.0) - 2.9957323 * jax.random.uniform(keys[0], (S, L, NX, NY), jnp.float32) ** block_levels(keys[0], (S, L, NX, NY), ((0, 16), (2, 16), (3, 2)), -0.2, 0.2)), 0.05, 1.0)
    cotangent = gaussian(keys[1], (S, L, NX, NY), 1.0, 6.0, ((0, 16), (2, 16), (3, 2)), jnp.float32)
    growth_rate = jnp.clip(jnp.exp(math.log(10000.0) - 9.2103404 * jax.random.uniform(keys[2], (L, NX, NY), jnp.float32) ** block_levels(keys[2], (L, NX, NY), ((1, 16), (2, 2)), -0.2, 0.2)), 1.0, 10000.0)
    section_factor = jnp.clip(jnp.exp(jax.random.uniform(keys[3], (S,), jnp.float32, math.log(0.5), math.log(2.0))), 0.5, 2.0)
    velocity = jnp.clip(jax.random.uniform(keys[4], (2, L, NX, NY), jnp.float32, -1.0, 1.0) * block_levels(keys[4], (2, L, NX, NY), ((2, 16), (3, 2)), -0.4, 0.0), -1.0, 1.0)
    diffusivity = jnp.clip(jnp.exp(jax.random.uniform(keys[5], (S,), jnp.float32, math.log(0.05), math.log(0.4))), 0.05, 0.4)
    kernel = jnp.clip(jnp.exp(jax.random.uniform(keys[6], (S, S), jnp.float32, math.log(0.001), math.log(0.03))), 0.001, 0.03)
    target = draw_target(jax.random.fold_in(keys[8], 71), 0)
    return {"number": number, "cotangent": cotangent, "growth_rate": growth_rate, "section_factor": section_factor, "velocity": velocity, "diffusivity": diffusivity, "kernel": kernel, "target": target}


step_size = 0.25
vertical_mix = 0.2
highest = lax.Precision.HIGHEST


def vertical(field):
    widths = [(0, 0)] * (field.ndim - 3) + [(1, 1), (0, 0), (0, 0)]
    extended = jnp.pad(field, widths, mode="edge")
    return extended[..., 2:, :, :] + extended[..., :-2, :, :] - 2.0 * field


def neighbours(field):
    return (jnp.roll(field, -1, 2), jnp.roll(field, 1, 2), jnp.roll(field, -1, 3), jnp.roll(field, 1, 3))


def reference(number, cotangent, growth_rate, section_factor, velocity, diffusivity, kernel, target):
    diffusion = diffusivity[:, None, None, None]
    x_plus, x_minus, y_plus, y_minus = neighbours(number)
    advected = (-velocity[0] * (x_plus - x_minus) * 0.5 - velocity[1] * (y_plus - y_minus) * 0.5
                + diffusion * (x_plus + x_minus + y_plus + y_minus - 4.0 * number)
                + vertical_mix * vertical(number))
    cell_count = L * NX * NY
    growth_step = step_size * (growth_rate[None] * section_factor[:, None, None, None]).reshape(S, cell_count)
    prior_step = jnp.concatenate([jnp.zeros((1, cell_count), jnp.float32), growth_step[:-1]], axis=0)
    flat_number = number.reshape(S, cell_count)
    flat_cot = cotangent.reshape(S, cell_count)

    def backward(carried, inputs):
        source, growth = inputs
        value = (source + growth * carried) / (1.0 + growth)
        return value, value

    _, adjoint = lax.scan(backward, jnp.zeros((cell_count,), jnp.float32), (flat_cot, growth_step), reverse=True)

    def pairing(carried, inputs):
        gain_sum, spread = carried
        kernel_row, target_row, number_row = inputs
        half_row = 0.5 * kernel_row
        produced = half_row[:, None] * flat_number * number_row[None, :]
        gain_sum = gain_sum + jax.ops.segment_sum(produced, target_row, num_segments=S)
        lookup = half_row[:, None] * adjoint[target_row]
        own_row = jnp.sum(lookup * flat_number, axis=0)
        spread = spread + lookup * number_row[None, :]
        return (gain_sum, spread), own_row

    zero_field = jnp.zeros((S, cell_count), jnp.float32)
    (gain_sum, spread), own_rows = lax.scan(pairing, (zero_field, zero_field), (kernel, target, flat_number))
    pull = jnp.dot(kernel, flat_number, precision=highest)
    loss_rows = flat_number * pull
    loss_adjoint = -adjoint * pull - jnp.dot(kernel.T, adjoint * flat_number, precision=highest)
    explicit = flat_number + step_size * (advected.reshape(S, cell_count) + gain_sum - loss_rows)

    def forward(carried, inputs):
        source, prior, growth = inputs
        value = (source + prior * carried) / (1.0 + growth)
        return value, value

    _, number_next = lax.scan(forward, jnp.zeros((cell_count,), jnp.float32), (explicit, prior_step, growth_step))
    adjoint_grid = adjoint.reshape(number.shape)
    flux_x = velocity[0] * adjoint_grid
    flux_y = velocity[1] * adjoint_grid
    a_xp, a_xm, a_yp, a_ym = neighbours(adjoint_grid)
    transported = ((jnp.roll(flux_x, -1, 2) - jnp.roll(flux_x, 1, 2)) * 0.5
                   + (jnp.roll(flux_y, -1, 3) - jnp.roll(flux_y, 1, 3)) * 0.5
                   + diffusion * (a_xp + a_xm + a_yp + a_ym - 4.0 * adjoint_grid)
                   + vertical_mix * vertical(adjoint_grid))
    gradient = adjoint + step_size * (transported.reshape(S, cell_count) + own_rows + spread + loss_adjoint)
    return number_next.reshape(number.shape), gradient.reshape(number.shape)
```

```python
import functools

import jax
import jax.numpy as jnp
from jax import lax
from jax.experimental import pallas as pl
from jax.experimental.pallas import tpu as pltpu
from jax.sharding import PartitionSpec as P

step_size = 0.25
vertical_mix = 0.2
highest = lax.Precision.HIGHEST
f32 = jnp.float32
bf16 = jnp.bfloat16

S = 128
B = 16
R = 8
L = 4
X = 8
Y = 128
GROUP = 16
PER = 4

INV, FWD, FWD_PI, BWD, BWD_PI = (256 * i for i in range(5))
FWD_Q, BWD_Q = 1280, 1408
COEF_ROWS = 1536

vmem = pl.BlockSpec(memory_space=pltpu.VMEM)
smem = pl.BlockSpec(memory_space=pltpu.SMEM)


def row_offsets():
    offsets, at = [], 0
    for group in range(S // GROUP):
        offsets.append(at)
        at += GROUP * (S - GROUP * group)
    return offsets, at


OFFSETS, WEIGHT_ROWS = row_offsets()


def call(kernel, outs, in_specs, name, flops=0, nbytes=1 << 20, scratch=(), limit=None):
    single = not isinstance(outs, (tuple, list))
    return pl.pallas_call(
        kernel,
        out_shape=outs,
        in_specs=in_specs,
        out_specs=vmem if single else [vmem] * len(outs),
        scratch_shapes=list(scratch),
        name=name,
        cost_estimate=pl.CostEstimate(flops=flops, bytes_accessed=nbytes, transcendentals=0),
        compiler_params=pltpu.CompilerParams(vmem_limit_bytes=limit or (32 << 20)),
    )


def shape(*dims, dtype=f32):
    return jax.ShapeDtypeStruct(dims, dtype)


def pack_y(tiles):
    lane = lax.broadcasted_iota(jnp.int32, (X, Y), 1)
    packed = jnp.zeros((X, Y), f32)
    for i, tile in enumerate(tiles):
        packed = jnp.where(lane // 2 == i, pltpu.roll(tile, 2 * i + 1, 1), packed)
    return packed


def pack_kernel(n_ref, c_ref, vel_ref, send_ref, low_ref, high_ref, y_ref):
    for m in range(L * X):
        send_ref[pl.ds(m * 16, 8), :] = n_ref[pl.ds(m, R, stride=L * X), :]
        send_ref[pl.ds(m * 16 + 8, 8), :] = c_ref[pl.ds(m, R, stride=L * X), :]
    for ref, row in ((low_ref, 0), (high_ref, X - 1)):
        ref[pl.ds(0, 32), :] = n_ref[pl.ds(row, 32, stride=X), :]
        edge = jnp.concatenate(
            [vel_ref[pl.ds(l * X + row, 1), :] for l in range(L)] + [jnp.zeros((4, Y), f32)], axis=0
        )
        ref[pl.ds(32, 8), :] = edge
    tiles = [n_ref[pl.ds(i * X, X), :] for i in range(R * L)]
    tiles += [vel_ref[pl.ds(32 + l * X, X), :] for l in range(L)]
    y_ref[...] = pack_y(tiles)


def shifted(tile, below, above, packed, i, masks):
    first_row, last_row, first_lane, last_lane = masks
    x_plus = jnp.where(last_row, above, pltpu.roll(tile, X - 1, 0))
    x_minus = jnp.where(first_row, below, pltpu.roll(tile, 1, 0))
    y_plus = jnp.where(last_lane, pltpu.roll(packed, 126 - 2 * i, 1), pltpu.roll(tile, Y - 1, 1))
    low = packed if i == 0 else pltpu.roll(packed, Y - 2 * i, 1)
    y_minus = jnp.where(first_lane, low, pltpu.roll(tile, 1, 1))
    return x_plus, x_minus, y_plus, y_minus


def edge_masks():
    row = lax.broadcasted_iota(jnp.int32, (X, Y), 0)
    lane = lax.broadcasted_iota(jnp.int32, (X, Y), 1)
    return row == 0, row == X - 1, lane == 0, lane == Y - 1


def vertical(column, l):
    return column[min(l + 1, L - 1)] + column[max(l - 1, 0)] - 2.0 * column[l]


def forward_kernel(
    n_ref, below_ref, above_ref, y_ref, vel_ref, rate_ref, factor_ref, diff_ref, local_ref, end_ref
):
    first = lax.axis_index("sec") * R
    masks = edge_masks()
    packed = y_ref[...]
    before = [jnp.zeros((X, Y), f32) for _ in range(L)]
    for s in range(R):
        column = [n_ref[pl.ds((s * L + l) * X, X), :] for l in range(L)]
        diffusion = diff_ref[first + s]
        factor = factor_ref[first + s]
        prior_factor = jnp.where(first + s == 0, 0.0, factor_ref[jnp.maximum(first + s - 1, 0)])
        for l in range(L):
            i = s * L + l
            u = vel_ref[pl.ds(l * X, X), :]
            w = vel_ref[pl.ds(32 + l * X, X), :]
            v = column[l]
            xp, xm, yp, ym = shifted(
                v, below_ref[pl.ds(i, 1), :], above_ref[pl.ds(i, 1), :], packed, i, masks
            )
            moved = (
                -u * (xp - xm) * 0.5
                - w * (yp - ym) * 0.5
                + diffusion * (xp + xm + yp + ym - 4.0 * v)
                + vertical_mix * vertical(column, l)
            )
            rate = rate_ref[pl.ds(l * X, X), :]
            growth = step_size * (rate * factor)
            prior = step_size * (rate * prior_factor)
            value = (v + step_size * moved + prior * before[l]) / (1.0 + growth)
            before[l] = value
            local_ref[pl.ds(i * X, X), :] = value
    for l in range(L):
        end_ref[pl.ds(l * X, X), :] = before[l]


def adjoint_kernel(c_ref, mid_ref, rate_ref, factor_ref, adj_ref, low_ref, high_ref, y_ref):
    first = lax.axis_index("sec") * R
    carried = []
    for l in range(L):
        even = mid_ref[pl.ds(l * 16, 4, stride=4), :]
        odd = mid_ref[pl.ds(l * 16 + 1, 4, stride=4), :]
        carried.append(
            jnp.concatenate(
                [part[k : k + 1] for k in range(4) for part in (even, odd)], axis=0
            )
        )
    tiles = [None] * (R * L)
    for s in reversed(range(R)):
        factor = factor_ref[first + s]
        for l in range(L):
            growth = step_size * (rate_ref[pl.ds(l * X, X), :] * factor)
            value = (c_ref[pl.ds((s * L + l) * X, X), :] + growth * carried[l]) / (1.0 + growth)
            carried[l] = value
            tiles[s * L + l] = value
            adj_ref[pl.ds((s * L + l) * X, X), :] = value
    low_ref[...] = adj_ref[pl.ds(0, 32, stride=X), :]
    high_ref[...] = adj_ref[pl.ds(X - 1, 32, stride=X), :]
    y_ref[...] = pack_y(tiles)


def gradient_kernel(
    adj_ref, below_ref, above_ref, y_ref, vel_ref, vel_below_ref, vel_above_ref, vel_y_ref, diff_ref, out_ref
):
    first = lax.axis_index("sec") * R
    masks = edge_masks()
    packed = y_ref[...]
    winds = []
    for l in range(L):
        u = vel_ref[pl.ds(l * X, X), :]
        w = vel_ref[pl.ds(32 + l * X, X), :]
        edge = (vel_below_ref[pl.ds(32 + l, 1), :], vel_above_ref[pl.ds(32 + l, 1), :])
        up, um, _, _ = shifted(u, *edge, vel_y_ref[...], 32 + l, masks)
        _, _, wp, wm = shifted(w, *edge, vel_y_ref[...], 32 + l, masks)
        winds.append((up * 0.5, um * 0.5, wp * 0.5, wm * 0.5))
    for s in range(R):
        column = [adj_ref[pl.ds((s * L + l) * X, X), :] for l in range(L)]
        diffusion = diff_ref[first + s]
        for l in range(L):
            i = s * L + l
            v = column[l]
            xp, xm, yp, ym = shifted(
                v, below_ref[pl.ds(i, 1), :], above_ref[pl.ds(i, 1), :], packed, i, masks
            )
            up, um, wp, wm = winds[l]
            moved = (
                (up * xp - um * xm)
                + (wp * yp - wm * ym)
                + diffusion * (xp + xm + yp + ym - 4.0 * v)
                + vertical_mix * vertical(column, l)
            )
            out_ref[pl.ds(i * X, X), :] = v + step_size * moved


def final_kernel(back_ref, local_ref, part_ref, next_ref, gradient_ref):
    for s in range(R):
        for l in range(L):
            rows = pl.ds((s * L + l) * X, X)
            next_ref[rows, :] = local_ref[rows, :] + back_ref[pl.ds(l * 128 + s, X, stride=16), :]
            gradient_ref[rows, :] = (
                part_ref[rows, :] + step_size * back_ref[pl.ds(l * 128 + 8 + s, X, stride=16), :]
            )


def weight_kernel(
    kernel_ref, target_ref, factor_ref, rate_ref, weight_ref, turned_ref, coef_ref, rows_ref, column_ref
):
    kernel = kernel_ref[...]
    target = target_ref[...].astype(f32)
    turned = kernel.T
    target_turned = target.T
    turned_ref[...] = turned
    same = target == target_turned
    one = 0.5 * kernel + jnp.where(same, 0.5 * turned, 0.0)
    two = jnp.where(same, 0.0, 0.5 * turned)
    one_high = one.astype(bf16).astype(f32)
    two_high = two.astype(bf16).astype(f32)
    for i, part in enumerate(
        (target, target_turned, one_high, one - one_high, two_high, two - two_high)
    ):
        rows_ref[pl.ds(i * S, S), :] = part

    for group in range(S // GROUP):
        low = group * GROUP
        count = S - low
        ids = (lax.broadcasted_iota(jnp.int32, (count, S), 0) + low).astype(f32)

        def build(k, _, low=low, count=count, ids=ids, start=OFFSETS[group]):
            t1, t2, h1, l1, h2, l2 = (rows_ref[pl.ds(i * S + low + k, 1), :] for i in range(6))
            hit1, hit2 = ids == t1, ids == t2
            high = jnp.where(hit1, h1, jnp.where(hit2, h2, 0.0)).astype(bf16)
            rest = jnp.where(hit1, l1, jnp.where(hit2, l2, 0.0)).astype(bf16)
            rows = pl.ds(pl.multiple_of(start + k * count, 16), count)
            weight_ref[rows, :] = jnp.concatenate([high, rest], axis=1)
            return 0

        lax.fori_loop(0, GROUP, build, 0)

    device = lax.axis_index("sec")
    column_ref[...] = jnp.broadcast_to(factor_ref[...], (S, S)).T
    block = lax.broadcasted_iota(jnp.int32, (B, Y), 0)
    for r in range(2):
        rate = rate_ref[pl.ds(2 * device + r, 1), :]
        growths, inverses = [], []
        for i in range(R):
            growth = step_size * (rate * column_ref[pl.ds(i, B, stride=R), :])
            inverse = 1.0 / (1.0 + growth)
            coef_ref[pl.ds(INV + (i * 2 + r) * B, B), :] = inverse
            growths.append(growth)
            inverses.append(inverse)
        product = None
        for i in range(R):
            if i == 0:
                prior = jnp.where(block == 0, 0.0, pltpu.roll(growths[R - 1], 1, 0))
            else:
                prior = growths[i - 1]
            ratio = prior * inverses[i]
            product = ratio if product is None else ratio * product
            coef_ref[pl.ds(FWD + (i * 2 + r) * B, B), :] = ratio
            coef_ref[pl.ds(FWD_PI + (i * 2 + r) * B, B), :] = product
        q = jnp.where(block == 0, 0.0, product)
        for turn, hop in enumerate((1, 2, 4, 8)):
            coef_ref[pl.ds(FWD_Q + (turn * 2 + r) * B, B), :] = q
            q = q * pltpu.roll(q, hop, 0)
        product = None
        for i in reversed(range(R)):
            ratio = growths[i] * inverses[i]
            product = ratio if product is None else ratio * product
            coef_ref[pl.ds(BWD + (i * 2 + r) * B, B), :] = ratio
            coef_ref[pl.ds(BWD_PI + (i * 2 + r) * B, B), :] = product
        q = jnp.where(block == B - 1, 0.0, product)
        for turn, hop in enumerate((1, 2, 4, 8)):
            coef_ref[pl.ds(BWD_Q + (turn * 2 + r) * B, B), :] = q
            q = q * pltpu.roll(q, B - hop, 0)


def cell_adjoint_kernel(got_ref, coef_ref, end_ref, adj_ref, mid_ref):
    block = lax.broadcasted_iota(jnp.int32, (B, Y), 0)
    for r in range(2):
        value = None
        values = []
        for i in reversed(range(R)):
            at = (i * 2 + r) * B
            source = got_ref[pl.ds(r * 16 + 8 + i, B, stride=32), :] * coef_ref[pl.ds(INV + at, B), :]
            value = source if value is None else source + coef_ref[pl.ds(BWD + at, B), :] * value
            values.append((i, value))
        for turn, hop in enumerate((1, 2, 4, 8)):
            q = coef_ref[pl.ds(BWD_Q + (turn * 2 + r) * B, B), :]
            value = value + q * pltpu.roll(value, B - hop, 0)
        carry = jnp.where(block == B - 1, 0.0, pltpu.roll(value, B - 1, 0))
        for i, local in values:
            full = local + coef_ref[pl.ds(BWD_PI + (i * 2 + r) * B, B), :] * carry
            adj_ref[pl.ds(r * S + i, B, stride=R), :] = full
        mid_ref[pl.ds(r, B, stride=4), :] = carry
        mid_ref[pl.ds(2 + r, B, stride=4), :] = end_ref[pl.ds(r, B, stride=2), :]


def split(value):
    high = value.astype(bf16)
    return high, (value - high.astype(f32)).astype(bf16)


def pair_kernel(
    got_ref, adj_ref, weight_ref, kernel_ref, turned_ref, gain_out, coag_out, n_ref, a_ref, gain_ref, part_ref
):
    for r in range(2):
        for b in range(B):
            n_ref[pl.ds(b * 8, 8), pl.ds(r * Y, Y)] = got_ref[pl.ds(b * 32 + r * 16, 8), :]
        a_ref[:, pl.ds(r * Y, Y)] = adj_ref[pl.ds(r * S, S), :]
    number = n_ref[...]
    high, rest = split(number)
    right = jnp.concatenate([high, high, rest], axis=0)
    gain_ref[...] = jnp.zeros_like(gain_ref)

    for group in range(S // GROUP):
        low = group * GROUP
        count = S - low

        def visit(turn, _, low=low, count=count, start=OFFSETS[group]):
            rows = pl.ds(pl.multiple_of(start + turn * (PER * count), 16), PER * count)
            left = weight_ref[rows, :]
            left = jnp.concatenate([left, left[:, :S]], axis=1)
            found = jnp.dot(left, right, preferred_element_type=f32).reshape(PER, count, 2 * Y)
            total = gain_ref[pl.ds(low, count), :]
            adjoint = a_ref[pl.ds(low, count), :]
            for p in range(PER):
                k = low + turn * PER + p
                total = total + found[p] * n_ref[pl.ds(k, 1), :]
                share = (found[p] * adjoint).reshape(count // 8, 8, 2 * Y).sum(axis=0)
                for r in range(2):
                    rows = pl.ds(pl.multiple_of(r * 8 * S + k * 8, 8), 8)
                    part_ref[rows, :] = share[:, r * Y : (r + 1) * Y]
            gain_ref[pl.ds(low, count), :] = total
            return 0

        lax.fori_loop(0, GROUP // PER, visit, 0)

    adjoint = a_ref[...]
    pull = jnp.dot(kernel_ref[...], number, precision=highest, preferred_element_type=f32)
    back = jnp.dot(turned_ref[...], adjoint * number, precision=highest, preferred_element_type=f32)
    gain = step_size * (0.5 * gain_ref[...] - number * pull)
    for r in range(2):
        gain_out[pl.ds(r * S, S), :] = gain[:, r * Y : (r + 1) * Y]
    other = adjoint * pull + back
    for r in range(2):
        coag = part_ref[pl.ds(r * 8 * S, S, stride=8), :]
        for j in range(1, 8):
            coag = coag + part_ref[pl.ds(r * 8 * S + j, S, stride=8), :]
        coag_out[pl.ds(r * S, S), :] = coag - other[:, r * Y : (r + 1) * Y]


def cell_next_kernel(gain_ref, coag_ref, mid_ref, coef_ref, send_ref):
    block = lax.broadcasted_iota(jnp.int32, (B, Y), 0)
    for r in range(2):
        value = None
        values = []
        for i in range(R):
            at = (i * 2 + r) * B
            source = gain_ref[pl.ds(r * S + i, B, stride=R), :] * coef_ref[pl.ds(INV + at, B), :]
            value = source if value is None else source + coef_ref[pl.ds(FWD + at, B), :] * value
            values.append(value)
        value = value + mid_ref[pl.ds(2 + r, B, stride=4), :]
        for turn, hop in enumerate((1, 2, 4, 8)):
            q = coef_ref[pl.ds(FWD_Q + (turn * 2 + r) * B, B), :]
            value = value + q * pltpu.roll(value, hop, 0)
        carry = jnp.where(block == 0, 0.0, pltpu.roll(value, 1, 0))
        for i in range(R):
            full = values[i] + coef_ref[pl.ds(FWD_PI + (i * 2 + r) * B, B), :] * carry
            send_ref[pl.ds(r * 16 + i, B, stride=32), :] = full
        for b in range(B):
            send_ref[pl.ds(b * 32 + r * 16 + 8, 8), :] = coag_ref[pl.ds(r * S + b * 8, 8), :]


def exchange(rows):
    count = rows.shape[0]
    parts = lax.all_to_all(
        rows.reshape(B, count // B, Y), "sec", split_axis=0, concat_axis=0, tiled=True
    )
    return parts.reshape(count, Y)


def halo(low, high, packed):
    count = lax.axis_size("gx")
    up = [(i, (i + 1) % count) for i in range(count)]
    down = [(target, source) for source, target in up]
    below = lax.ppermute(high, "gx", up)
    above = lax.ppermute(low, "gx", down)
    other = lax.ppermute(packed, "gy", [(0, 1), (1, 0)])
    return below, above, other


def per_device(
    number, cotangent, growth_rate, section_factor, velocity, diffusivity, kernel, target
):
    n = number.reshape(256, Y)
    c = cotangent.reshape(256, Y)
    rate = growth_rate.reshape(32, Y)
    vel = velocity.reshape(64, Y)
    send, low, high, packed = call(
        pack_kernel,
        (shape(512, Y), shape(40, Y), shape(40, Y), shape(X, Y)),
        [vmem] * 3,
        "pack",
    )(n, c, vel)
    got = exchange(send)
    below, above, other = halo(low, high, packed)
    weight, turned, coef = call(
        weight_kernel,
        (shape(WEIGHT_ROWS, 2 * S, dtype=bf16), shape(S, S), shape(COEF_ROWS, Y)),
        [vmem] * 4,
        "weights",
        flops=1 << 20,
        nbytes=6 << 20,
        scratch=(pltpu.VMEM((6 * S, S), f32), pltpu.VMEM((S, S), f32)),
    )(kernel, target, section_factor.reshape(1, S), rate)
    local, ends = call(
        forward_kernel,
        (shape(256, Y), shape(32, Y)),
        [vmem] * 6 + [smem] * 2,
        "forward",
    )(n, below, above, other, vel, rate, section_factor, diffusivity)
    adj, mid = call(
        cell_adjoint_kernel, (shape(256, Y), shape(64, Y)), [vmem] * 3, "cell_adjoint"
    )(got, coef, ends)
    mid_got = exchange(mid)
    gain, coag = call(
        pair_kernel,
        (shape(256, Y), shape(256, Y)),
        [vmem] * 5,
        "pairs",
        flops=1 << 32,
        nbytes=8 << 20,
        scratch=(
            pltpu.VMEM((S, 2 * Y), f32),
            pltpu.VMEM((S, 2 * Y), f32),
            pltpu.VMEM((S, 2 * Y), f32),
            pltpu.VMEM((2 * S * 8, Y), f32),
        ),
    )(got, adj, weight, kernel, turned)
    send_back = call(cell_next_kernel, shape(512, Y), [vmem] * 4, "cell_next")(
        gain, coag, mid_got, coef
    )
    back = exchange(send_back)
    adj_own, a_low, a_high, a_packed = call(
        adjoint_kernel,
        (shape(256, Y), shape(32, Y), shape(32, Y), shape(X, Y)),
        [vmem] * 3 + [smem],
        "adjoint",
    )(c, mid_got, rate, section_factor)
    a_below, a_above, a_other = halo(a_low, a_high, a_packed)
    part = call(gradient_kernel, shape(256, Y), [vmem] * 8 + [smem], "gradient")(
        adj_own, a_below, a_above, a_other, vel, below, above, other, diffusivity
    )
    next_rows, gradient = call(
        final_kernel, (shape(256, Y), shape(256, Y)), [vmem] * 3, "final"
    )(back, local, part)
    return next_rows.reshape(number.shape), gradient.reshape(number.shape)


def solution(mesh):
    return jax.shard_map(
        per_device,
        mesh=mesh,
        in_specs=(
            P("sec", None, "gx", "gy"),
            P("sec", None, "gx", "gy"),
            P(None, "gx", "gy"),
            P(),
            P(None, None, "gx", "gy"),
            P(),
            P(),
            P(),
        ),
        out_specs=(P("sec", None, "gx", "gy"), P("sec", None, "gx", "gy")),
        check_vma=False,
    )
```

```python
import jax
import jax.numpy as jnp
from jax import lax
from jax.experimental import pallas as pl
from jax.experimental.pallas import tpu as pltpu
from jax.sharding import PartitionSpec as P

step_size = 0.25
vertical_mix = 0.2
highest = lax.Precision.HIGHEST
f32 = jnp.float32
bf16 = jnp.bfloat16

S = 128
B = 16
R = 8
L = 4
X = 8
Y = 128
GROUP = 16
PER = 4

INV, FWD, FWD_PI = (256 * i for i in range(3))
FWD_Q = 768
COEF_ROWS = 896
EDGE_ROWS = S + 8

vmem = pl.BlockSpec(memory_space=pltpu.VMEM)
hbm = pl.BlockSpec(memory_space=pltpu.HBM)


def row_offsets():
    offsets, at = [], 0
    for group in range(S // GROUP):
        offsets.append(at)
        at += GROUP * (S - GROUP * group)
    return offsets, at


OFFSETS, WEIGHT_ROWS = row_offsets()


def call(kernel, outs, in_specs, name, flops=0, nbytes=1 << 20, scratch=(), limit=None):
    single = not isinstance(outs, (tuple, list))
    return pl.pallas_call(
        kernel,
        out_shape=outs,
        in_specs=in_specs,
        out_specs=vmem if single else [vmem] * len(outs),
        scratch_shapes=list(scratch),
        name=name,
        cost_estimate=pl.CostEstimate(flops=flops, bytes_accessed=nbytes, transcendentals=0),
        compiler_params=pltpu.CompilerParams(vmem_limit_bytes=limit or (32 << 20)),
    )


def shape(*dims, dtype=f32):
    return jax.ShapeDtypeStruct(dims, dtype)


def swap_groups(tiles):
    group = lax.broadcasted_iota(jnp.int32, (8, Y), 1) // 8
    tiles = list(tiles)
    for bit in (1, 2, 4, 8):
        upper = (group & bit) != 0
        for i in range(B):
            if i & bit == 0:
                a, b = tiles[i], tiles[i | bit]
                tiles[i] = jnp.where(upper, pltpu.roll(b, 8 * bit, 1), a)
                tiles[i | bit] = jnp.where(upper, b, pltpu.roll(a, Y - 8 * bit, 1))
    return tiles


def own_cells(rows, device):
    shift = lax.rem(Y - 8 * device, Y)
    moved = pltpu.roll(pltpu.roll(rows, shift, 1), 0, 1, stride=8, stride_axis=0)
    group = lax.broadcasted_iota(jnp.int32, (B, Y), 1) // 8
    row = lax.broadcasted_iota(jnp.int32, (B, Y), 0)
    return jnp.sum(jnp.where(group == row, moved, 0.0), axis=0, keepdims=True)


def pack_kernel(
    n_hbm, c_hbm, rate_hbm, vel_hbm, factor_hbm, diff_hbm, kernel_hbm, target_hbm,
    send_ref, own_ref, factor_ref, diff_ref, kernel_ref, target_ref,
    n_ref, c_ref, rate_ref, vel_ref, row_ref, sems,
):
    device = lax.axis_index("sec")
    pairs = (
        (n_hbm, n_ref),
        (c_hbm, c_ref),
        (rate_hbm, rate_ref),
        (vel_hbm, vel_ref),
        (factor_hbm, row_ref.at[pl.ds(0, 1)]),
        (diff_hbm, row_ref.at[pl.ds(8, 1)]),
        (kernel_hbm, kernel_ref),
        (target_hbm, target_ref),
    )
    copies = [pltpu.make_async_copy(a, b, sems.at[i]) for i, (a, b) in enumerate(pairs)]
    for copy in copies:
        copy.start()
    for array, ref in enumerate((n_ref, c_ref)):
        copies[array].wait()
        for half in range(2):
            tiles = swap_groups(
                ref[pl.ds(half * 16 + g, R, stride=L * X), :] for g in range(B)
            )
            for d, tile in enumerate(tiles):
                send_ref[pl.ds(d * 32 + array * 16 + half * 8, 8), :] = tile
    for copy in copies[2:]:
        copy.wait()
    rows = [own_cells(rate_ref[pl.ds(h * 16, 16), :], device) for h in range(2)]
    rows += [own_cells(vel_ref[pl.ds(h * 16, 16), :], device) for h in range(4)]
    own_ref[...] = jnp.concatenate(rows + [jnp.zeros((2, Y), f32)], axis=0)
    factor_ref[...] = jnp.broadcast_to(row_ref[pl.ds(0, 1), :], (S, S)).T
    diff_ref[...] = jnp.broadcast_to(row_ref[pl.ds(8, 1), :], (S, S)).T


def lane_parts():
    lane = lax.broadcasted_iota(jnp.int32, (8, Y), 1)
    return lane // 64, (lane // 8) % 8, lane % 8


def turn(tile, shift):
    shift = shift % Y
    return tile if shift == 0 else pltpu.roll(tile, shift, 1)


def pack_edges(tiles, which, refs, rows):
    _, x, y = which
    x_up, x_down, y_up, y_down = (jnp.zeros((8, Y), f32) for _ in range(4))
    for i, tile in enumerate(tiles):
        x_up = jnp.where(x == i, turn(tile, 8 * (i - 7)), x_up)
        x_down = jnp.where(x == 7 - i, turn(tile, 8 * (7 - i)), x_down)
        y_up = jnp.where(y == i, turn(tile, i - 7), y_up)
        y_down = jnp.where(y == 7 - i, turn(tile, 7 - i), y_down)
    for ref, edge in zip(refs, (x_up, x_down, y_up, y_down)):
        ref[rows, :] = edge


def shifted(tile, edges, i, which):
    _, x, y = which
    from_low_x, from_high_x, from_low_y, from_high_y = edges
    x_minus = jnp.where(x == 0, turn(from_low_x, -8 * i), turn(tile, 8))
    x_plus = jnp.where(x == 7, turn(from_high_x, 8 * i), turn(tile, -8))
    y_minus = jnp.where(y == 0, turn(from_low_y, -i), turn(tile, 1))
    y_plus = jnp.where(y == 7, turn(from_high_y, i), turn(tile, -1))
    return x_plus, x_minus, y_plus, y_minus


def vertical(low, high, which):
    first = which[0] == 0
    a, b = turn(low, 64), turn(high, 64)
    return (
        a + jnp.where(first, low, b) - 2.0 * low,
        b + jnp.where(first, a, high) - 2.0 * high,
    )


def adjoint_kernel(
    got_ref, own_ref, factor_ref, adj_ref, coef_ref, x_up_ref, x_down_ref, y_up_ref, y_down_ref
):
    block = lax.broadcasted_iota(jnp.int32, (B, Y), 0)
    for h in range(2):
        rate = own_ref[pl.ds(h, 1), :]
        growths, inverses = [], []
        for i in range(R):
            growth = step_size * (rate * factor_ref[pl.ds(i, B, stride=R), :])
            inverse = 1.0 / (1.0 + growth)
            coef_ref[pl.ds(INV + (i * 2 + h) * B, B), :] = inverse
            growths.append(growth)
            inverses.append(inverse)
        product = None
        for i in range(R):
            prior = growths[i - 1] if i else jnp.where(block == 0, 0.0, pltpu.roll(growths[R - 1], 1, 0))
            ratio = prior * inverses[i]
            product = ratio if product is None else ratio * product
            coef_ref[pl.ds(FWD + (i * 2 + h) * B, B), :] = ratio
            coef_ref[pl.ds(FWD_PI + (i * 2 + h) * B, B), :] = product
        q = jnp.where(block == 0, 0.0, product)
        for turns, hop in enumerate((1, 2, 4, 8)):
            coef_ref[pl.ds(FWD_Q + (turns * 2 + h) * B, B), :] = q
            q = q * pltpu.roll(q, hop, 0)
        value, product, values = None, None, []
        for i in reversed(range(R)):
            source = got_ref[pl.ds(16 + h * 8 + i, B, stride=32), :] * inverses[i]
            ratio = growths[i] * inverses[i]
            value = source if value is None else source + ratio * value
            product = ratio if product is None else ratio * product
            values.append((i, value, product))
        q = jnp.where(block == B - 1, 0.0, product)
        for hop in (1, 2, 4, 8):
            value = value + q * pltpu.roll(value, B - hop, 0)
            q = q * pltpu.roll(q, B - hop, 0)
        carry = jnp.where(block == B - 1, 0.0, pltpu.roll(value, B - 1, 0))
        for i, local, product in values:
            adj_ref[pl.ds(h * S + i, B, stride=R), :] = local + product * carry
    which = lane_parts()
    refs = (x_up_ref, x_down_ref, y_up_ref, y_down_ref)
    for b in range(B):
        tiles = [got_ref[pl.ds(b * 32 + h * 8, 8), :] for h in range(2)]
        tiles += [adj_ref[pl.ds(h * S + b * 8, 8), :] for h in range(2)]
        pack_edges(tiles, which, refs, pl.ds(b * 8, 8))
    winds = [jnp.broadcast_to(own_ref[pl.ds(2 + h, 1), :], (8, Y)) for h in range(4)]
    pack_edges(winds, which, refs, pl.ds(S, 8))


def split(value):
    high = value.astype(bf16)
    return high, (value - high.astype(f32)).astype(bf16)


def pair_kernel(
    got_ref, adj_ref, kernel_ref, target_ref, gain_out, coag_out,
    n_ref, a_ref, gain_ref, part_ref, weight_ref, rows_ref,
):
    kernel = kernel_ref[...]
    target = target_ref[...].astype(f32)
    turned = kernel.T
    target_turned = target.T
    same = target == target_turned
    one = 0.5 * kernel + jnp.where(same, 0.5 * turned, 0.0)
    two = jnp.where(same, 0.0, 0.5 * turned)
    one_high = one.astype(bf16).astype(f32)
    two_high = two.astype(bf16).astype(f32)
    for i, part in enumerate(
        (target, target_turned, one_high, one - one_high, two_high, two - two_high)
    ):
        rows_ref[pl.ds(i * S, S), :] = part

    for group in range(S // GROUP):
        low = group * GROUP
        count = S - low
        ids = (lax.broadcasted_iota(jnp.int32, (count, S), 0) + low).astype(f32)

        def build(k, _, low=low, count=count, ids=ids, start=OFFSETS[group]):
            t1, t2, h1, l1, h2, l2 = (rows_ref[pl.ds(i * S + low + k, 1), :] for i in range(6))
            hit1, hit2 = ids == t1, ids == t2
            high = jnp.where(hit1, h1, jnp.where(hit2, h2, 0.0)).astype(bf16)
            rest = jnp.where(hit1, l1, jnp.where(hit2, l2, 0.0)).astype(bf16)
            rows = pl.ds(pl.multiple_of(start + k * count, 16), count)
            weight_ref[rows, :] = jnp.concatenate([high, rest], axis=1)
            return 0

        lax.fori_loop(0, GROUP, build, 0)

    for r in range(2):
        for b in range(B):
            n_ref[pl.ds(b * 8, 8), pl.ds(r * Y, Y)] = got_ref[pl.ds(b * 32 + r * 8, 8), :]
        a_ref[:, pl.ds(r * Y, Y)] = adj_ref[pl.ds(r * S, S), :]
    number = n_ref[...]
    high, rest = split(number)
    right = jnp.concatenate([high, high, rest], axis=0)
    gain_ref[...] = jnp.zeros_like(gain_ref)

    for group in range(S // GROUP):
        low = group * GROUP
        count = S - low

        def visit(turns, _, low=low, count=count, start=OFFSETS[group]):
            rows = pl.ds(pl.multiple_of(start + turns * (PER * count), 16), PER * count)
            left = weight_ref[rows, :]
            left = jnp.concatenate([left, left[:, :S]], axis=1)
            found = jnp.dot(left, right, preferred_element_type=f32).reshape(PER, count, 2 * Y)
            total = gain_ref[pl.ds(low, count), :]
            adjoint = a_ref[pl.ds(low, count), :]
            for p in range(PER):
                k = low + turns * PER + p
                total = total + found[p] * n_ref[pl.ds(k, 1), :]
                share = (found[p] * adjoint).reshape(count // 8, 8, 2 * Y).sum(axis=0)
                for r in range(2):
                    rows = pl.ds(pl.multiple_of(r * 8 * S + k * 8, 8), 8)
                    part_ref[rows, :] = share[:, r * Y : (r + 1) * Y]
            gain_ref[pl.ds(low, count), :] = total
            return 0

        lax.fori_loop(0, GROUP // PER, visit, 0)

    adjoint = a_ref[...]
    pull = jnp.dot(kernel, number, precision=highest, preferred_element_type=f32)
    back = jnp.dot(turned, adjoint * number, precision=highest, preferred_element_type=f32)
    gain = step_size * (0.5 * gain_ref[...] - number * pull)
    for r in range(2):
        gain_out[pl.ds(r * S, S), :] = gain[:, r * Y : (r + 1) * Y]
    other = adjoint * pull + back
    for r in range(2):
        coag = part_ref[pl.ds(r * 8 * S, S, stride=8), :]
        for j in range(1, 8):
            coag = coag + part_ref[pl.ds(r * 8 * S + j, S, stride=8), :]
        coag_out[pl.ds(r * S, S), :] = coag - other[:, r * Y : (r + 1) * Y]


def next_kernel(
    got_ref, adj_ref, own_ref, diff_ref, coef_ref, gain_ref, coag_ref,
    low_x_ref, high_x_ref, low_y_ref, high_y_ref, send_ref, right_ref,
):
    which = lane_parts()
    refs = (low_x_ref, high_x_ref, low_y_ref, high_y_ref)
    wind_edges = [ref[pl.ds(S, 8), :] for ref in refs]
    winds = []
    for h in range(2):
        u = jnp.broadcast_to(own_ref[pl.ds(2 + h, 1), :], (8, Y))
        w = jnp.broadcast_to(own_ref[pl.ds(4 + h, 1), :], (8, Y))
        up, um, _, _ = shifted(u, wind_edges, h, which)
        _, _, wp, wm = shifted(w, wind_edges, 2 + h, which)
        winds.append((0.5 * u, 0.5 * w, 0.5 * up, 0.5 * um, 0.5 * wp, 0.5 * wm))
    for b in range(B):
        edges = [ref[pl.ds(b * 8, 8), :] for ref in refs]
        diffusion = diff_ref[pl.ds(b * 8, 8), :]
        numbers = [got_ref[pl.ds(b * 32 + h * 8, 8), :] for h in range(2)]
        adjoints = [adj_ref[pl.ds(h * S + b * 8, 8), :] for h in range(2)]
        number_levels = vertical(*numbers, which)
        adjoint_levels = vertical(*adjoints, which)
        for h in range(2):
            u, w, up, um, wp, wm = winds[h]
            rows = pl.ds(h * S + b * 8, 8)
            v = numbers[h]
            xp, xm, yp, ym = shifted(v, edges, h, which)
            moved = (
                diffusion * (xp + xm + yp + ym - 4.0 * v)
                - u * (xp - xm)
                - w * (yp - ym)
                + vertical_mix * number_levels[h]
            )
            right_ref[rows, :] = v + step_size * moved + gain_ref[rows, :]
            v = adjoints[h]
            xp, xm, yp, ym = shifted(v, edges, 2 + h, which)
            moved = (
                diffusion * (xp + xm + yp + ym - 4.0 * v)
                + (up * xp - um * xm)
                + (wp * yp - wm * ym)
                + vertical_mix * adjoint_levels[h]
            )
            send_ref[pl.ds(b * 32 + 16 + h * 8, 8), :] = v + step_size * (moved + coag_ref[rows, :])
    block = lax.broadcasted_iota(jnp.int32, (B, Y), 0)
    for h in range(2):
        value, values = None, []
        for i in range(R):
            at = (i * 2 + h) * B
            source = right_ref[pl.ds(h * S + i, B, stride=R), :] * coef_ref[pl.ds(INV + at, B), :]
            value = source if value is None else source + coef_ref[pl.ds(FWD + at, B), :] * value
            values.append(value)
        for turns, hop in enumerate((1, 2, 4, 8)):
            q = coef_ref[pl.ds(FWD_Q + (turns * 2 + h) * B, B), :]
            value = value + q * pltpu.roll(value, hop, 0)
        carry = jnp.where(block == 0, 0.0, pltpu.roll(value, 1, 0))
        for i in range(R):
            full = values[i] + coef_ref[pl.ds(FWD_PI + (i * 2 + h) * B, B), :] * carry
            send_ref[pl.ds(h * 8 + i, B, stride=32), :] = full


def unpack_kernel(back_ref, next_ref, gradient_ref):
    for array, ref in enumerate((next_ref, gradient_ref)):
        for half in range(2):
            tiles = swap_groups(
                back_ref[pl.ds(d * 32 + array * 16 + half * 8, 8), :] for d in range(B)
            )
            for g, tile in enumerate(tiles):
                ref[pl.ds(half * 16 + g, R, stride=L * X), :] = tile


def exchange(rows):
    count = rows.shape[0]
    parts = lax.all_to_all(
        rows.reshape(B, count // B, Y), "sec", split_axis=0, concat_axis=0, tiled=True
    )
    return parts.reshape(count, Y)


def ring(count, place=lambda i: i, back=False):
    steps = [(place(i), place((i + 1) % count)) for i in range(count)]
    return [(target, source) for source, target in steps] if back else steps


def y_place(position):
    return position % B * 2 + position // B


def per_device(
    number, cotangent, growth_rate, section_factor, velocity, diffusivity, kernel, target
):
    send, own, factor, diff, kernel_in, target_in = call(
        pack_kernel,
        (
            shape(512, Y), shape(8, Y), shape(S, S), shape(S, S), shape(S, S),
            shape(S, S, dtype=jnp.int32),
        ),
        [hbm] * 8,
        "pack",
        scratch=(
            pltpu.VMEM((256, Y), f32),
            pltpu.VMEM((256, Y), f32),
            pltpu.VMEM((32, Y), f32),
            pltpu.VMEM((64, Y), f32),
            pltpu.VMEM((16, Y), f32),
            pltpu.SemaphoreType.DMA((8,)),
        ),
    )(
        number.reshape(256, Y),
        cotangent.reshape(256, Y),
        growth_rate.reshape(32, Y),
        velocity.reshape(64, Y),
        section_factor.reshape(1, S),
        diffusivity.reshape(1, S),
        kernel,
        target,
    )
    got = exchange(send)
    adj, coef, x_up, x_down, y_up, y_down = call(
        adjoint_kernel,
        (shape(256, Y), shape(COEF_ROWS, Y)) + (shape(EDGE_ROWS, Y),) * 4,
        [vmem] * 3,
        "adjoint",
    )(got, own, factor)
    x_count = lax.axis_size("gx")
    edges = (
        lax.ppermute(x_up, "gx", ring(x_count)),
        lax.ppermute(x_down, "gx", ring(x_count, back=True)),
        lax.ppermute(y_up, ("sec", "gy"), ring(2 * B, y_place)),
        lax.ppermute(y_down, ("sec", "gy"), ring(2 * B, y_place, True)),
    )
    gain, coag = call(
        pair_kernel,
        (shape(256, Y), shape(256, Y)),
        [vmem] * 4,
        "pairs",
        flops=1 << 32,
        nbytes=8 << 20,
        scratch=(
            pltpu.VMEM((S, 2 * Y), f32),
            pltpu.VMEM((S, 2 * Y), f32),
            pltpu.VMEM((S, 2 * Y), f32),
            pltpu.VMEM((2 * S * 8, Y), f32),
            pltpu.VMEM((WEIGHT_ROWS, 2 * S), bf16),
            pltpu.VMEM((6 * S, S), f32),
        ),
    )(got, adj, kernel_in, target_in)
    send_back = call(
        next_kernel, shape(512, Y), [vmem] * 11, "next", scratch=(pltpu.VMEM((256, Y), f32),)
    )(got, adj, own, diff, coef, gain, coag, *edges)
    next_rows, gradient = call(
        unpack_kernel, (shape(256, Y), shape(256, Y)), [vmem], "unpack"
    )(exchange(send_back))
    return next_rows.reshape(number.shape), gradient.reshape(number.shape)


def solution(mesh):
    return jax.shard_map(
        per_device,
        mesh=mesh,
        in_specs=(
            P("sec", None, "gx", "gy"),
            P("sec", None, "gx", "gy"),
            P(None, "gx", "gy"),
            P(),
            P(None, None, "gx", "gy"),
            P(),
            P(),
            P(),
        ),
        out_specs=(P("sec", None, "gx", "gy"), P("sec", None, "gx", "gy")),
        check_vma=False,
    )
```

```python
import jax
import jax.numpy as jnp
from jax import lax
from jax.experimental import pallas as pl
from jax.experimental.pallas import tpu as pltpu
from jax.sharding import PartitionSpec as P

step_size = 0.25
vertical_mix = 0.2
highest = lax.Precision.HIGHEST
f32 = jnp.float32
bf16 = jnp.bfloat16

S = 128
B = 16
R = 8
L = 4
X = 8
Y = 128
GROUP = 16

INV, FWD, FWD_PI = (256 * i for i in range(3))
FWD_Q = 768
COEF_ROWS = 896
EDGE_ROWS = S + 8

vmem = pl.BlockSpec(memory_space=pltpu.VMEM)
hbm = pl.BlockSpec(memory_space=pltpu.HBM)


def row_offsets():
    offsets, at = [], 0
    for group in range(S // GROUP):
        offsets.append(at)
        at += GROUP * (S - GROUP * group)
    return offsets, at


OFFSETS, WEIGHT_ROWS = row_offsets()


def call(kernel, outs, in_specs, name, flops=0, nbytes=1 << 20, scratch=(), limit=None):
    single = not isinstance(outs, (tuple, list))
    return pl.pallas_call(
        kernel,
        out_shape=outs,
        in_specs=in_specs,
        out_specs=vmem if single else [vmem] * len(outs),
        scratch_shapes=list(scratch),
        name=name,
        cost_estimate=pl.CostEstimate(flops=flops, bytes_accessed=nbytes, transcendentals=0),
        compiler_params=pltpu.CompilerParams(vmem_limit_bytes=limit or (32 << 20)),
    )


def shape(*dims, dtype=f32):
    return jax.ShapeDtypeStruct(dims, dtype)


def swap_groups(tiles):
    group = lax.broadcasted_iota(jnp.int32, (8, Y), 1) // 8
    tiles = list(tiles)
    for bit in (1, 2, 4, 8):
        upper = (group & bit) != 0
        for i in range(B):
            if i & bit == 0:
                a, b = tiles[i], tiles[i | bit]
                tiles[i] = jnp.where(upper, pltpu.roll(b, 8 * bit, 1), a)
                tiles[i | bit] = jnp.where(upper, b, pltpu.roll(a, Y - 8 * bit, 1))
    return tiles


def run_of(index):
    return jnp.where(lax.axis_index("gy") == 0, index, B - 1 - index)


def own_cells(rows, run):
    shift = lax.rem(Y - 8 * run, Y)
    moved = pltpu.roll(pltpu.roll(rows, shift, 1), 0, 1, stride=8, stride_axis=0)
    group = lax.broadcasted_iota(jnp.int32, (B, Y), 1) // 8
    row = lax.broadcasted_iota(jnp.int32, (B, Y), 0)
    return jnp.sum(jnp.where(group == row, moved, 0.0), axis=0, keepdims=True)


def pack_kernel(
    n_hbm, c_hbm, rate_hbm, vel_hbm, factor_hbm, diff_hbm, kernel_hbm, target_hbm,
    send_ref, own_ref, factor_ref, diff_ref, kernel_ref, target_ref,
    n_ref, c_ref, rate_ref, vel_ref, row_ref, sems,
):
    run = run_of(lax.axis_index("sec"))
    pairs = (
        (n_hbm, n_ref),
        (c_hbm, c_ref),
        (rate_hbm, rate_ref),
        (vel_hbm, vel_ref),
        (factor_hbm, row_ref.at[pl.ds(0, 1)]),
        (diff_hbm, row_ref.at[pl.ds(8, 1)]),
        (kernel_hbm, kernel_ref),
        (target_hbm, target_ref),
    )
    copies = [pltpu.make_async_copy(a, b, sems.at[i]) for i, (a, b) in enumerate(pairs)]
    for copy in copies:
        copy.start()
    for array, ref in enumerate((n_ref, c_ref)):
        copies[array].wait()
        for half in range(2):
            tiles = swap_groups(
                ref[pl.ds(half * 16 + g, R, stride=L * X), :] for g in range(B)
            )
            for d, tile in enumerate(tiles):
                at = pl.multiple_of(run_of(d) * 32 + array * 16 + half * 8, 8)
                send_ref[pl.ds(at, 8), :] = tile
    for copy in copies[2:]:
        copy.wait()
    rows = [own_cells(rate_ref[pl.ds(h * 16, 16), :], run) for h in range(2)]
    rows += [own_cells(vel_ref[pl.ds(h * 16, 16), :], run) for h in range(4)]
    own_ref[...] = jnp.concatenate(rows + [jnp.zeros((2, Y), f32)], axis=0)
    factor_ref[...] = jnp.broadcast_to(row_ref[pl.ds(0, 1), :], (S, S)).T
    diff_ref[...] = jnp.broadcast_to(row_ref[pl.ds(8, 1), :], (S, S)).T


def lane_parts():
    lane = lax.broadcasted_iota(jnp.int32, (8, Y), 1)
    return lane // 64, (lane // 8) % 8, lane % 8


def turn(tile, shift):
    shift = shift % Y
    return tile if shift == 0 else pltpu.roll(tile, shift, 1)


def even_places():
    return lax.rem(lax.axis_index("gx"), 2) == 0, lax.rem(run_of(lax.axis_index("sec")), 2) == 0


def pack_edges(tiles, which, even, refs, rows):
    _, x, y = which
    x_up, x_down, y_up, y_down = (jnp.zeros((8, Y), f32) for _ in range(4))
    for i, tile in enumerate(tiles):
        x_up = jnp.where(x == i, turn(tile, 8 * (i - 7)), x_up)
        x_down = jnp.where(x == 7 - i, turn(tile, 8 * (7 - i)), x_down)
        y_up = jnp.where(y == i, turn(tile, i - 7), y_up)
        y_down = jnp.where(y == 7 - i, turn(tile, 7 - i), y_down)
    for i, (up, down) in enumerate(((x_up, x_down), (y_up, y_down))):
        refs[2 * i][rows, :] = jnp.where(even[i], up, down)
        refs[2 * i + 1][rows, :] = jnp.where(even[i], down, up)


def received_edges(even, refs, rows):
    edges = []
    for i in range(2):
        a, b = (ref[rows, :] for ref in refs[2 * i : 2 * i + 2])
        edges += [jnp.where(even[i], b, a), jnp.where(even[i], a, b)]
    return edges


def shifted(tile, edges, i, which):
    _, x, y = which
    from_low_x, from_high_x, from_low_y, from_high_y = edges
    x_minus = jnp.where(x == 0, turn(from_low_x, -8 * i), turn(tile, 8))
    x_plus = jnp.where(x == 7, turn(from_high_x, 8 * i), turn(tile, -8))
    y_minus = jnp.where(y == 0, turn(from_low_y, -i), turn(tile, 1))
    y_plus = jnp.where(y == 7, turn(from_high_y, i), turn(tile, -1))
    return x_plus, x_minus, y_plus, y_minus


def vertical(low, high, which):
    first = which[0] == 0
    a, b = turn(low, 64), turn(high, 64)
    return (
        a + jnp.where(first, low, b) - 2.0 * low,
        b + jnp.where(first, a, high) - 2.0 * high,
    )


def adjoint_kernel(
    got_ref, own_ref, factor_ref, adj_ref, coef_ref, x_first_ref, x_second_ref, y_first_ref, y_second_ref
):
    block = lax.broadcasted_iota(jnp.int32, (B, Y), 0)
    for h in range(2):
        rate = own_ref[pl.ds(h, 1), :]
        growths, inverses = [], []
        for i in range(R):
            growth = step_size * (rate * factor_ref[pl.ds(i, B, stride=R), :])
            inverse = 1.0 / (1.0 + growth)
            coef_ref[pl.ds(INV + (i * 2 + h) * B, B), :] = inverse
            growths.append(growth)
            inverses.append(inverse)
        product = None
        for i in range(R):
            prior = growths[i - 1] if i else jnp.where(block == 0, 0.0, pltpu.roll(growths[R - 1], 1, 0))
            ratio = prior * inverses[i]
            product = ratio if product is None else ratio * product
            coef_ref[pl.ds(FWD + (i * 2 + h) * B, B), :] = ratio
            coef_ref[pl.ds(FWD_PI + (i * 2 + h) * B, B), :] = product
        q = jnp.where(block == 0, 0.0, product)
        for turns, hop in enumerate((1, 2, 4, 8)):
            coef_ref[pl.ds(FWD_Q + (turns * 2 + h) * B, B), :] = q
            q = q * pltpu.roll(q, hop, 0)
        value, product, values = None, None, []
        for i in reversed(range(R)):
            source = got_ref[pl.ds(16 + h * 8 + i, B, stride=32), :] * inverses[i]
            ratio = growths[i] * inverses[i]
            value = source if value is None else source + ratio * value
            product = ratio if product is None else ratio * product
            values.append((i, value, product))
        q = jnp.where(block == B - 1, 0.0, product)
        for hop in (1, 2, 4, 8):
            value = value + q * pltpu.roll(value, B - hop, 0)
            q = q * pltpu.roll(q, B - hop, 0)
        carry = jnp.where(block == B - 1, 0.0, pltpu.roll(value, B - 1, 0))
        for i, local, product in values:
            adj_ref[pl.ds(h * S + i, B, stride=R), :] = local + product * carry
    which = lane_parts()
    even = even_places()
    refs = (x_first_ref, x_second_ref, y_first_ref, y_second_ref)
    for b in range(B):
        tiles = [got_ref[pl.ds(b * 32 + h * 8, 8), :] for h in range(2)]
        tiles += [adj_ref[pl.ds(h * S + b * 8, 8), :] for h in range(2)]
        pack_edges(tiles, which, even, refs, pl.ds(b * 8, 8))
    winds = [jnp.broadcast_to(own_ref[pl.ds(2 + h, 1), :], (8, Y)) for h in range(4)]
    pack_edges(winds, which, even, refs, pl.ds(S, 8))


def split(value):
    high = value.astype(bf16)
    return high, (value - high.astype(f32)).astype(bf16)


def pair_kernel(
    got_ref, adj_ref, kernel_ref, target_ref, gain_out, coag_out,
    n_ref, a_ref, gain_ref, part_ref, weight_ref, rows_ref,
):
    kernel = kernel_ref[...]
    target = target_ref[...].astype(f32)
    turned = kernel.T
    target_turned = target.T
    same = target == target_turned
    one = 0.5 * kernel + jnp.where(same, 0.5 * turned, 0.0)
    two = jnp.where(same, 0.0, 0.5 * turned)
    one_high = one.astype(bf16).astype(f32)
    two_high = two.astype(bf16).astype(f32)
    for i, part in enumerate(
        (target, target_turned, one_high, one - one_high, two_high, two - two_high)
    ):
        rows_ref[pl.ds(i * S, S), :] = part

    for group in range(S // GROUP):
        low = group * GROUP
        count = S - low
        ids = (lax.broadcasted_iota(jnp.int32, (count, S), 0) + low).astype(f32)

        def build(k, _, low=low, count=count, ids=ids, start=OFFSETS[group]):
            t1, t2, h1, l1, h2, l2 = (rows_ref[pl.ds(i * S + low + k, 1), :] for i in range(6))
            hit1, hit2 = ids == t1, ids == t2
            high = jnp.where(hit1, h1, jnp.where(hit2, h2, 0.0)).astype(bf16)
            rest = jnp.where(hit1, l1, jnp.where(hit2, l2, 0.0)).astype(bf16)
            rows = pl.ds(pl.multiple_of(start + k * count, 16), count)
            weight_ref[rows, :] = jnp.concatenate([high, rest], axis=1)
            return 0

        lax.fori_loop(0, GROUP, build, 0, unroll=True)

    for r in range(2):
        for b in range(B):
            n_ref[pl.ds(b * 8, 8), pl.ds(r * Y, Y)] = got_ref[pl.ds(b * 32 + r * 8, 8), :]
        a_ref[:, pl.ds(r * Y, Y)] = adj_ref[pl.ds(r * S, S), :]
    number = n_ref[...]
    high, rest = split(number)
    right = jnp.concatenate([high, high, rest], axis=0)
    gain_ref[...] = jnp.zeros_like(gain_ref)

    for group in range(S // GROUP):
        low = group * GROUP
        count = S - low

        left = weight_ref[pl.ds(OFFSETS[group], GROUP * count), :]
        left = jnp.concatenate([left, left[:, :S]], axis=1)
        found = jnp.dot(left, right, preferred_element_type=f32).reshape(GROUP, count, 2 * Y)
        total = gain_ref[pl.ds(low, count), :]
        adjoint = a_ref[pl.ds(low, count), :]
        for p in range(GROUP):
            k = low + p
            total = total + found[p] * n_ref[pl.ds(k, 1), :]
            share = (found[p] * adjoint).reshape(count // 8, 8, 2 * Y).sum(axis=0)
            for r in range(2):
                part_ref[pl.ds(r * 8 * S + k * 8, 8), :] = share[:, r * Y : (r + 1) * Y]
        gain_ref[pl.ds(low, count), :] = total

    adjoint = a_ref[...]
    pull = jnp.dot(kernel, number, precision=highest, preferred_element_type=f32)
    back = jnp.dot(turned, adjoint * number, precision=highest, preferred_element_type=f32)
    gain = step_size * (0.5 * gain_ref[...] - number * pull)
    for r in range(2):
        gain_out[pl.ds(r * S, S), :] = gain[:, r * Y : (r + 1) * Y]
    other = adjoint * pull + back
    for r in range(2):
        coag = part_ref[pl.ds(r * 8 * S, S, stride=8), :]
        for j in range(1, 8):
            coag = coag + part_ref[pl.ds(r * 8 * S + j, S, stride=8), :]
        coag_out[pl.ds(r * S, S), :] = coag - other[:, r * Y : (r + 1) * Y]


def next_kernel(
    got_ref, adj_ref, own_ref, diff_ref, coef_ref, gain_ref, coag_ref,
    x_first_ref, x_second_ref, y_first_ref, y_second_ref, send_ref, right_ref,
):
    which = lane_parts()
    even = even_places()
    refs = (x_first_ref, x_second_ref, y_first_ref, y_second_ref)
    wind_edges = received_edges(even, refs, pl.ds(S, 8))
    winds = []
    for h in range(2):
        u = jnp.broadcast_to(own_ref[pl.ds(2 + h, 1), :], (8, Y))
        w = jnp.broadcast_to(own_ref[pl.ds(4 + h, 1), :], (8, Y))
        up, um, _, _ = shifted(u, wind_edges, h, which)
        _, _, wp, wm = shifted(w, wind_edges, 2 + h, which)
        winds.append((0.5 * u, 0.5 * w, 0.5 * up, 0.5 * um, 0.5 * wp, 0.5 * wm))
    for b in range(B):
        edges = received_edges(even, refs, pl.ds(b * 8, 8))
        diffusion = diff_ref[pl.ds(b * 8, 8), :]
        numbers = [got_ref[pl.ds(b * 32 + h * 8, 8), :] for h in range(2)]
        adjoints = [adj_ref[pl.ds(h * S + b * 8, 8), :] for h in range(2)]
        number_levels = vertical(*numbers, which)
        adjoint_levels = vertical(*adjoints, which)
        for h in range(2):
            u, w, up, um, wp, wm = winds[h]
            rows = pl.ds(h * S + b * 8, 8)
            v = numbers[h]
            xp, xm, yp, ym = shifted(v, edges, h, which)
            moved = (
                diffusion * (xp + xm + yp + ym - 4.0 * v)
                - u * (xp - xm)
                - w * (yp - ym)
                + vertical_mix * number_levels[h]
            )
            right_ref[rows, :] = v + step_size * moved + gain_ref[rows, :]
            v = adjoints[h]
            xp, xm, yp, ym = shifted(v, edges, 2 + h, which)
            moved = (
                diffusion * (xp + xm + yp + ym - 4.0 * v)
                + (up * xp - um * xm)
                + (wp * yp - wm * ym)
                + vertical_mix * adjoint_levels[h]
            )
            send_ref[pl.ds(b * 32 + 16 + h * 8, 8), :] = v + step_size * (moved + coag_ref[rows, :])
    block = lax.broadcasted_iota(jnp.int32, (B, Y), 0)
    for h in range(2):
        value, values = None, []
        for i in range(R):
            at = (i * 2 + h) * B
            source = right_ref[pl.ds(h * S + i, B, stride=R), :] * coef_ref[pl.ds(INV + at, B), :]
            value = source if value is None else source + coef_ref[pl.ds(FWD + at, B), :] * value
            values.append(value)
        for turns, hop in enumerate((1, 2, 4, 8)):
            q = coef_ref[pl.ds(FWD_Q + (turns * 2 + h) * B, B), :]
            value = value + q * pltpu.roll(value, hop, 0)
        carry = jnp.where(block == 0, 0.0, pltpu.roll(value, 1, 0))
        for i in range(R):
            full = values[i] + coef_ref[pl.ds(FWD_PI + (i * 2 + h) * B, B), :] * carry
            send_ref[pl.ds(h * 8 + i, B, stride=32), :] = full


def unpack_kernel(back_ref, next_ref, gradient_ref):
    for array, ref in enumerate((next_ref, gradient_ref)):
        for half in range(2):
            tiles = swap_groups(
                back_ref[pl.ds(pl.multiple_of(run_of(d) * 32 + array * 16 + half * 8, 8), 8), :]
                for d in range(B)
            )
            for g, tile in enumerate(tiles):
                ref[pl.ds(half * 16 + g, R, stride=L * X), :] = tile


def exchange(rows):
    count = rows.shape[0]
    parts = lax.all_to_all(
        rows.reshape(B, count // B, Y), "sec", split_axis=0, concat_axis=0, tiled=True
    )
    return parts.reshape(count, Y)


def swaps(count, first, place=lambda i: i):
    pairs = [(place(i), place((i + 1) % count)) for i in range(first, count, 2)]
    return pairs + [(b, a) for a, b in pairs]


def y_place(position):
    half, run = position // B, position % B
    return (B - 1 - run if half else run) * 2 + half


def per_device(
    number, cotangent, growth_rate, section_factor, velocity, diffusivity, kernel, target
):
    send, own, factor, diff, kernel_in, target_in = call(
        pack_kernel,
        (
            shape(512, Y), shape(8, Y), shape(S, S), shape(S, S), shape(S, S),
            shape(S, S, dtype=jnp.int32),
        ),
        [hbm] * 8,
        "pack",
        scratch=(
            pltpu.VMEM((256, Y), f32),
            pltpu.VMEM((256, Y), f32),
            pltpu.VMEM((32, Y), f32),
            pltpu.VMEM((64, Y), f32),
            pltpu.VMEM((16, Y), f32),
            pltpu.SemaphoreType.DMA((8,)),
        ),
    )(
        *(
            pltpu.with_memory_space_constraint(array, pltpu.HBM)
            for array in (
                number.reshape(256, Y),
                cotangent.reshape(256, Y),
                growth_rate.reshape(32, Y),
                velocity.reshape(64, Y),
                section_factor.reshape(1, S),
                diffusivity.reshape(1, S),
                kernel,
                target,
            )
        )
    )
    got = exchange(send)
    adj, coef, x_first, x_second, y_first, y_second = call(
        adjoint_kernel,
        (shape(256, Y), shape(COEF_ROWS, Y)) + (shape(EDGE_ROWS, Y),) * 4,
        [vmem] * 3,
        "adjoint",
    )(got, own, factor)
    x_count = lax.axis_size("gx")
    edges = (
        lax.ppermute(x_first, "gx", swaps(x_count, 0)),
        lax.ppermute(x_second, "gx", swaps(x_count, 1)),
        lax.ppermute(y_first, ("sec", "gy"), swaps(2 * B, 0, y_place)),
        lax.ppermute(y_second, ("sec", "gy"), swaps(2 * B, 1, y_place)),
    )
    gain, coag = call(
        pair_kernel,
        (shape(256, Y), shape(256, Y)),
        [vmem] * 4,
        "pairs",
        flops=1 << 32,
        nbytes=8 << 20,
        scratch=(
            pltpu.VMEM((S, 2 * Y), f32),
            pltpu.VMEM((S, 2 * Y), f32),
            pltpu.VMEM((S, 2 * Y), f32),
            pltpu.VMEM((2 * S * 8, Y), f32),
            pltpu.VMEM((WEIGHT_ROWS, 2 * S), bf16),
            pltpu.VMEM((6 * S, S), f32),
        ),
    )(got, adj, kernel_in, target_in)
    send_back = call(
        next_kernel, shape(512, Y), [vmem] * 11, "next", scratch=(pltpu.VMEM((256, Y), f32),)
    )(got, adj, own, diff, coef, gain, coag, *edges)
    next_rows, gradient = call(
        unpack_kernel, (shape(256, Y), shape(256, Y)), [vmem], "unpack"
    )(exchange(send_back))
    return next_rows.reshape(number.shape), gradient.reshape(number.shape)


def solution(mesh):
    return jax.shard_map(
        per_device,
        mesh=mesh,
        in_specs=(
            P("sec", None, "gx", "gy"),
            P("sec", None, "gx", "gy"),
            P(None, "gx", "gy"),
            P(),
            P(None, None, "gx", "gy"),
            P(),
            P(),
            P(),
        ),
        out_specs=(P("sec", None, "gx", "gy"), P("sec", None, "gx", "gy")),
        check_vma=False,
    )
```

```python
import jax
import jax.numpy as jnp
from jax import lax
from jax.experimental import pallas as pl
from jax.experimental.pallas import tpu as pltpu
from jax.sharding import PartitionSpec as P

step_size = 0.25
vertical_mix = 0.2
highest = lax.Precision.HIGHEST
f32 = jnp.float32
bf16 = jnp.bfloat16

S = 128
B = 16
R = 8
L = 4
X = 8
Y = 128
GROUP = 16

INV, FWD, FWD_PI = (256 * i for i in range(3))
FWD_Q = 768
COEF_ROWS = 896
EDGE_ROWS = S + 8

vmem = pl.BlockSpec(memory_space=pltpu.VMEM)
hbm = pl.BlockSpec(memory_space=pltpu.HBM)


def row_offsets():
    offsets, at = [], 0
    for group in range(S // GROUP):
        offsets.append(at)
        at += GROUP * (S - GROUP * group)
    return offsets, at


OFFSETS, WEIGHT_ROWS = row_offsets()


def call(kernel, outs, in_specs, name, flops=0, nbytes=1 << 20, scratch=(), place=vmem):
    single = not isinstance(outs, (tuple, list))
    return pl.pallas_call(
        kernel,
        out_shape=outs,
        in_specs=in_specs,
        out_specs=place if single else [place] * len(outs),
        scratch_shapes=list(scratch),
        name=name,
        cost_estimate=pl.CostEstimate(flops=flops, bytes_accessed=nbytes, transcendentals=0),
        compiler_params=pltpu.CompilerParams(vmem_limit_bytes=32 << 20),
    )


def shape(*dims, dtype=f32):
    return jax.ShapeDtypeStruct(dims, dtype)


def swap_groups(tiles):
    group = lax.broadcasted_iota(jnp.int32, (8, Y), 1) // 8
    tiles = list(tiles)
    tiles = [tiles[-i % B] for i in range(B)]
    tiles = [pltpu.roll(tile, 8 * (-i % B), 1) if i else tile for i, tile in enumerate(tiles)]
    for bit in (1, 2, 4, 8):
        upper = (group & bit) != 0
        tiles = [jnp.where(upper, tiles[i - bit], tiles[i]) for i in range(B)]
    return [pltpu.roll(tile, Y - 8 * i, 1) if i else tile for i, tile in enumerate(tiles)]


def run_of(index):
    return jnp.where(lax.axis_index("gy") == 0, index, B - 1 - index)


def own_cells(rows, run):
    shift = lax.rem(Y - 8 * run, Y)
    moved = pltpu.roll(pltpu.roll(rows, shift, 1), 0, 1, stride=8, stride_axis=0)
    group = lax.broadcasted_iota(jnp.int32, (B, Y), 1) // 8
    row = lax.broadcasted_iota(jnp.int32, (B, Y), 0)
    return jnp.sum(jnp.where(group == row, moved, 0.0), axis=0, keepdims=True)


def pack_kernel(
    n_hbm, c_hbm, rate_hbm, vel_hbm, factor_hbm, diff_hbm, kernel_hbm, target_hbm,
    send_ref, own_ref, factor_ref, diff_ref, kernel_ref, target_ref,
    n_ref, c_ref, rate_ref, vel_ref, row_ref, sems,
):
    run = run_of(lax.axis_index("sec"))
    pairs = (
        (factor_hbm, row_ref.at[pl.ds(0, 1)]),
        (diff_hbm, row_ref.at[pl.ds(8, 1)]),
        (rate_hbm, rate_ref),
        (vel_hbm, vel_ref),
        (n_hbm, n_ref),
        (c_hbm, c_ref),
        (kernel_hbm, kernel_ref),
        (target_hbm, target_ref),
    )
    copies = [pltpu.make_async_copy(a, b, sems.at[i]) for i, (a, b) in enumerate(pairs)]
    for copy in copies:
        copy.start()
    for copy in copies[:4]:
        copy.wait()
    rows = [own_cells(rate_ref[pl.ds(h * 16, 16), :], run) for h in range(2)]
    rows += [own_cells(vel_ref[pl.ds(h * 16, 16), :], run) for h in range(4)]
    own_ref[...] = jnp.concatenate(rows + [jnp.zeros((2, Y), f32)], axis=0)
    factor_ref[...] = jnp.broadcast_to(row_ref[pl.ds(0, 1), :], (S, S)).T
    diff_ref[...] = jnp.broadcast_to(row_ref[pl.ds(8, 1), :], (S, S)).T
    for array, ref in enumerate((n_ref, c_ref)):
        copies[4 + array].wait()
        for half in range(2):
            tiles = swap_groups(
                ref[pl.ds(half * 16 + g, R, stride=L * X), :] for g in range(B)
            )
            for d, tile in enumerate(tiles):
                at = pl.multiple_of(run_of(d) * 32 + array * 16 + half * 8, 8)
                send_ref[pl.ds(at, 8), :] = tile
    for copy in copies[6:]:
        copy.wait()


def lane_parts():
    lane = lax.broadcasted_iota(jnp.int32, (8, Y), 1)
    return lane // 64, (lane // 8) % 8, lane % 8


def turn(tile, shift):
    shift = shift % Y
    return tile if shift == 0 else pltpu.roll(tile, shift, 1)


def even_places():
    return lax.rem(lax.axis_index("gx"), 2) == 0, lax.rem(run_of(lax.axis_index("sec")), 2) == 0


def pack_edges(tiles, which, even, refs, rows):
    _, x, y = which
    x_up, x_down, y_up, y_down = (jnp.zeros((8, Y), f32) for _ in range(4))
    for i, tile in enumerate(tiles):
        x_up = jnp.where(x == i, turn(tile, 8 * (i - 7)), x_up)
        x_down = jnp.where(x == 7 - i, turn(tile, 8 * (7 - i)), x_down)
        y_up = jnp.where(y == i, turn(tile, i - 7), y_up)
        y_down = jnp.where(y == 7 - i, turn(tile, 7 - i), y_down)
    for i, (up, down) in enumerate(((x_up, x_down), (y_up, y_down))):
        refs[2 * i][rows, :] = jnp.where(even[i], up, down)
        refs[2 * i + 1][rows, :] = jnp.where(even[i], down, up)


def received_edges(even, refs, rows):
    edges = []
    for i in range(2):
        a, b = (ref[rows, :] for ref in refs[2 * i : 2 * i + 2])
        edges += [jnp.where(even[i], b, a), jnp.where(even[i], a, b)]
    return edges


def shifted(tile, edges, i, which):
    _, x, y = which
    from_low_x, from_high_x, from_low_y, from_high_y = edges
    x_minus = jnp.where(x == 0, turn(from_low_x, -8 * i), turn(tile, 8))
    x_plus = jnp.where(x == 7, turn(from_high_x, 8 * i), turn(tile, -8))
    y_minus = jnp.where(y == 0, turn(from_low_y, -i), turn(tile, 1))
    y_plus = jnp.where(y == 7, turn(from_high_y, i), turn(tile, -1))
    return x_plus, x_minus, y_plus, y_minus


def vertical(low, high, which):
    first = which[0] == 0
    a, b = turn(low, 64), turn(high, 64)
    return (
        a + jnp.where(first, low, b) - 2.0 * low,
        b + jnp.where(first, a, high) - 2.0 * high,
    )


def adjoint_kernel(
    got_ref, own_ref, factor_ref, adj_ref, coef_ref, x_first_ref, x_second_ref, y_first_ref, y_second_ref
):
    block = lax.broadcasted_iota(jnp.int32, (B, Y), 0)
    for h in range(2):
        rate = own_ref[pl.ds(h, 1), :]
        growths, inverses = [], []
        for i in range(R):
            growth = step_size * (rate * factor_ref[pl.ds(i, B, stride=R), :])
            inverse = 1.0 / (1.0 + growth)
            coef_ref[pl.ds(INV + (i * 2 + h) * B, B), :] = inverse
            growths.append(growth)
            inverses.append(inverse)
        product = None
        for i in range(R):
            prior = growths[i - 1] if i else jnp.where(block == 0, 0.0, pltpu.roll(growths[R - 1], 1, 0))
            ratio = prior * inverses[i]
            product = ratio if product is None else ratio * product
            coef_ref[pl.ds(FWD + (i * 2 + h) * B, B), :] = ratio
            coef_ref[pl.ds(FWD_PI + (i * 2 + h) * B, B), :] = product
        q = jnp.where(block == 0, 0.0, product)
        for turns, hop in enumerate((1, 2, 4, 8)):
            coef_ref[pl.ds(FWD_Q + (turns * 2 + h) * B, B), :] = q
            q = q * pltpu.roll(q, hop, 0)
        value, product, values = None, None, []
        for i in reversed(range(R)):
            source = got_ref[pl.ds(16 + h * 8 + i, B, stride=32), :] * inverses[i]
            ratio = growths[i] * inverses[i]
            value = source if value is None else source + ratio * value
            product = ratio if product is None else ratio * product
            values.append((i, value, product))
        q = jnp.where(block == B - 1, 0.0, product)
        for hop in (1, 2, 4, 8):
            value = value + q * pltpu.roll(value, B - hop, 0)
            q = q * pltpu.roll(q, B - hop, 0)
        carry = jnp.where(block == B - 1, 0.0, pltpu.roll(value, B - 1, 0))
        for i, local, product in values:
            adj_ref[pl.ds(h * S + i, B, stride=R), :] = local + product * carry
    which = lane_parts()
    even = even_places()
    refs = (x_first_ref, x_second_ref, y_first_ref, y_second_ref)
    for b in range(B):
        tiles = [got_ref[pl.ds(b * 32 + h * 8, 8), :] for h in range(2)]
        tiles += [adj_ref[pl.ds(h * S + b * 8, 8), :] for h in range(2)]
        pack_edges(tiles, which, even, refs, pl.ds(b * 8, 8))
    winds = [jnp.broadcast_to(own_ref[pl.ds(2 + h, 1), :], (8, Y)) for h in range(4)]
    pack_edges(winds, which, even, refs, pl.ds(S, 8))


def split(value):
    high = value.astype(bf16)
    return high, (value - high.astype(f32)).astype(bf16)


def pair_kernel(
    got_ref, adj_ref, kernel_ref, target_ref, gain_out, coag_out,
    n_ref, a_ref, gain_ref, part_ref, weight_ref, rows_ref,
):
    kernel = kernel_ref[...]
    target = target_ref[...].astype(f32)
    turned = kernel.T
    target_turned = target.T
    same = target == target_turned
    one = 0.5 * kernel + jnp.where(same, 0.5 * turned, 0.0)
    two = jnp.where(same, 0.0, 0.5 * turned)
    one_high = one.astype(bf16).astype(f32)
    two_high = two.astype(bf16).astype(f32)
    for i, part in enumerate(
        (target, target_turned, one_high, one - one_high, two_high, two - two_high)
    ):
        rows_ref[pl.ds(i * S, S), :] = part

    for group in range(S // GROUP):
        low = group * GROUP
        count = S - low
        ids = (lax.broadcasted_iota(jnp.int32, (count, S), 0) + low).astype(f32)

        def build(k, _, low=low, count=count, ids=ids, start=OFFSETS[group]):
            t1, t2, h1, l1, h2, l2 = (rows_ref[pl.ds(i * S + low + k, 1), :] for i in range(6))
            hit1, hit2 = ids == t1, ids == t2
            high = jnp.where(hit1, h1, jnp.where(hit2, h2, 0.0)).astype(bf16)
            rest = jnp.where(hit1, l1, jnp.where(hit2, l2, 0.0)).astype(bf16)
            rows = pl.ds(pl.multiple_of(start + k * count, 16), count)
            weight_ref[rows, :] = jnp.concatenate([high, rest], axis=1)
            return 0

        lax.fori_loop(0, GROUP, build, 0, unroll=True)

    for r in range(2):
        for b in range(B):
            n_ref[pl.ds(b * 8, 8), pl.ds(r * Y, Y)] = got_ref[pl.ds(b * 32 + r * 8, 8), :]
        a_ref[:, pl.ds(r * Y, Y)] = adj_ref[pl.ds(r * S, S), :]
    number = n_ref[...]
    high, rest = split(number)
    right = jnp.concatenate([high, high, rest], axis=0)
    gain_ref[...] = jnp.zeros_like(gain_ref)

    for group in range(S // GROUP):
        low = group * GROUP
        count = S - low

        left = weight_ref[pl.ds(OFFSETS[group], GROUP * count), :]
        left = jnp.concatenate([left, left[:, :S]], axis=1)
        found = jnp.dot(left, right, preferred_element_type=f32).reshape(GROUP, count, 2 * Y)
        total = gain_ref[pl.ds(low, count), :]
        adjoint = a_ref[pl.ds(low, count), :]
        for p in range(GROUP):
            k = low + p
            total = total + found[p] * n_ref[pl.ds(k, 1), :]
            share = (found[p] * adjoint).reshape(count // 8, 8, 2 * Y).sum(axis=0)
            for r in range(2):
                part_ref[pl.ds(r * 8 * S + k * 8, 8), :] = share[:, r * Y : (r + 1) * Y]
        gain_ref[pl.ds(low, count), :] = total

    adjoint = a_ref[...]
    pull = jnp.dot(kernel, number, precision=highest, preferred_element_type=f32)
    back = jnp.dot(turned, adjoint * number, precision=highest, preferred_element_type=f32)
    gain = step_size * (0.5 * gain_ref[...] - number * pull)
    for r in range(2):
        gain_out[pl.ds(r * S, S), :] = gain[:, r * Y : (r + 1) * Y]
    other = adjoint * pull + back
    for r in range(2):
        coag = part_ref[pl.ds(r * 8 * S, S, stride=8), :]
        for j in range(1, 8):
            coag = coag + part_ref[pl.ds(r * 8 * S + j, S, stride=8), :]
        coag_out[pl.ds(r * S, S), :] = coag - other[:, r * Y : (r + 1) * Y]


def next_kernel(
    got_ref, adj_ref, own_ref, diff_ref, coef_ref, gain_ref, coag_ref,
    x_first_ref, x_second_ref, y_first_ref, y_second_ref, send_ref, right_ref,
):
    which = lane_parts()
    even = even_places()
    refs = (x_first_ref, x_second_ref, y_first_ref, y_second_ref)
    wind_edges = received_edges(even, refs, pl.ds(S, 8))
    winds = []
    for h in range(2):
        u = jnp.broadcast_to(own_ref[pl.ds(2 + h, 1), :], (8, Y))
        w = jnp.broadcast_to(own_ref[pl.ds(4 + h, 1), :], (8, Y))
        up, um, _, _ = shifted(u, wind_edges, h, which)
        _, _, wp, wm = shifted(w, wind_edges, 2 + h, which)
        winds.append((0.5 * u, 0.5 * w, 0.5 * up, 0.5 * um, 0.5 * wp, 0.5 * wm))
    for b in range(B):
        edges = received_edges(even, refs, pl.ds(b * 8, 8))
        diffusion = diff_ref[pl.ds(b * 8, 8), :]
        numbers = [got_ref[pl.ds(b * 32 + h * 8, 8), :] for h in range(2)]
        adjoints = [adj_ref[pl.ds(h * S + b * 8, 8), :] for h in range(2)]
        number_levels = vertical(*numbers, which)
        adjoint_levels = vertical(*adjoints, which)
        for h in range(2):
            u, w, up, um, wp, wm = winds[h]
            rows = pl.ds(h * S + b * 8, 8)
            v = numbers[h]
            xp, xm, yp, ym = shifted(v, edges, h, which)
            moved = (
                diffusion * (xp + xm + yp + ym - 4.0 * v)
                - u * (xp - xm)
                - w * (yp - ym)
                + vertical_mix * number_levels[h]
            )
            right_ref[rows, :] = v + step_size * moved + gain_ref[rows, :]
            v = adjoints[h]
            xp, xm, yp, ym = shifted(v, edges, 2 + h, which)
            moved = (
                diffusion * (xp + xm + yp + ym - 4.0 * v)
                + (up * xp - um * xm)
                + (wp * yp - wm * ym)
                + vertical_mix * adjoint_levels[h]
            )
            send_ref[pl.ds(b * 32 + 16 + h * 8, 8), :] = v + step_size * (moved + coag_ref[rows, :])
    block = lax.broadcasted_iota(jnp.int32, (B, Y), 0)
    for h in range(2):
        value, values = None, []
        for i in range(R):
            at = (i * 2 + h) * B
            source = right_ref[pl.ds(h * S + i, B, stride=R), :] * coef_ref[pl.ds(INV + at, B), :]
            value = source if value is None else source + coef_ref[pl.ds(FWD + at, B), :] * value
            values.append(value)
        for turns, hop in enumerate((1, 2, 4, 8)):
            q = coef_ref[pl.ds(FWD_Q + (turns * 2 + h) * B, B), :]
            value = value + q * pltpu.roll(value, hop, 0)
        carry = jnp.where(block == 0, 0.0, pltpu.roll(value, 1, 0))
        for i in range(R):
            full = values[i] + coef_ref[pl.ds(FWD_PI + (i * 2 + h) * B, B), :] * carry
            send_ref[pl.ds(h * 8 + i, B, stride=32), :] = full


def unpack_kernel(back_ref, next_hbm, gradient_hbm, next_ref, gradient_ref, sems):
    copies = []
    for array, (ref, out) in enumerate(((next_ref, next_hbm), (gradient_ref, gradient_hbm))):
        for half in range(2):
            tiles = swap_groups(
                back_ref[pl.ds(pl.multiple_of(run_of(d) * 32 + array * 16 + half * 8, 8), 8), :]
                for d in range(B)
            )
            for g, tile in enumerate(tiles):
                ref[pl.ds(half * 16 + g, R, stride=L * X), :] = tile
        copies.append(pltpu.make_async_copy(ref, out, sems.at[array]))
        copies[-1].start()
    for copy in copies:
        copy.wait()


def exchange(rows):
    count = rows.shape[0]
    parts = lax.all_to_all(
        rows.reshape(B, count // B, Y), "sec", split_axis=0, concat_axis=0, tiled=True
    )
    return parts.reshape(count, Y)


def swaps(count, first, place=lambda i: i):
    pairs = [(place(i), place((i + 1) % count)) for i in range(first, count, 2)]
    return pairs + [(b, a) for a, b in pairs]


def y_place(position):
    half, run = position // B, position % B
    return (B - 1 - run if half else run) * 2 + half


def per_device(
    number, cotangent, growth_rate, section_factor, velocity, diffusivity, kernel, target
):
    send, own, factor, diff, kernel_in, target_in = call(
        pack_kernel,
        (
            shape(512, Y), shape(8, Y), shape(S, S), shape(S, S), shape(S, S),
            shape(S, S, dtype=jnp.int32),
        ),
        [hbm] * 8,
        "pack",
        scratch=(
            pltpu.VMEM((256, Y), f32),
            pltpu.VMEM((256, Y), f32),
            pltpu.VMEM((32, Y), f32),
            pltpu.VMEM((64, Y), f32),
            pltpu.VMEM((16, Y), f32),
            pltpu.SemaphoreType.DMA((8,)),
        ),
    )(
        *(
            pltpu.with_memory_space_constraint(array, pltpu.HBM)
            for array in (
                number.reshape(256, Y),
                cotangent.reshape(256, Y),
                growth_rate.reshape(32, Y),
                velocity.reshape(64, Y),
                section_factor.reshape(1, S),
                diffusivity.reshape(1, S),
                kernel,
                target,
            )
        )
    )
    got = exchange(send)
    adj, coef, x_first, x_second, y_first, y_second = call(
        adjoint_kernel,
        (shape(256, Y), shape(COEF_ROWS, Y)) + (shape(EDGE_ROWS, Y),) * 4,
        [vmem] * 3,
        "adjoint",
    )(got, own, factor)
    x_count = lax.axis_size("gx")
    edges = (
        lax.ppermute(x_first, "gx", swaps(x_count, 0)),
        lax.ppermute(x_second, "gx", swaps(x_count, 1)),
        lax.ppermute(y_first, ("sec", "gy"), swaps(2 * B, 0, y_place)),
        lax.ppermute(y_second, ("sec", "gy"), swaps(2 * B, 1, y_place)),
    )
    gain, coag = call(
        pair_kernel,
        (shape(256, Y), shape(256, Y)),
        [vmem] * 4,
        "pairs",
        flops=1 << 32,
        nbytes=8 << 20,
        scratch=(
            pltpu.VMEM((S, 2 * Y), f32),
            pltpu.VMEM((S, 2 * Y), f32),
            pltpu.VMEM((S, 2 * Y), f32),
            pltpu.VMEM((2 * S * 8, Y), f32),
            pltpu.VMEM((WEIGHT_ROWS, 2 * S), bf16),
            pltpu.VMEM((6 * S, S), f32),
        ),
    )(got, adj, kernel_in, target_in)
    send_back = call(
        next_kernel, shape(512, Y), [vmem] * 11, "next", scratch=(pltpu.VMEM((256, Y), f32),)
    )(got, adj, own, diff, coef, gain, coag, *edges)
    next_rows, gradient = call(
        unpack_kernel,
        (shape(256, Y), shape(256, Y)),
        [vmem],
        "unpack",
        scratch=(
            pltpu.VMEM((256, Y), f32),
            pltpu.VMEM((256, Y), f32),
            pltpu.SemaphoreType.DMA((2,)),
        ),
        place=hbm,
    )(exchange(send_back))
    return next_rows.reshape(number.shape), gradient.reshape(number.shape)


def solution(mesh):
    return jax.shard_map(
        per_device,
        mesh=mesh,
        in_specs=(
            P("sec", None, "gx", "gy"),
            P("sec", None, "gx", "gy"),
            P(None, "gx", "gy"),
            P(),
            P(None, None, "gx", "gy"),
            P(),
            P(),
            P(),
        ),
        out_specs=(P("sec", None, "gx", "gy"), P("sec", None, "gx", "gy")),
        check_vma=False,
    )
```

```python
import jax
import jax.numpy as jnp
from jax import lax
from jax.experimental import pallas as pl
from jax.experimental.pallas import tpu as pltpu
from jax.sharding import PartitionSpec as P

step_size = 0.25
vertical_mix = 0.2
f32 = jnp.float32
bf16 = jnp.bfloat16

S = 128
B = 16
R = 8
L = 4
X = 8
Y = 128
GROUP = 16

INV, FWD, FWD_PI = (256 * i for i in range(3))
FWD_Q = 768
COEF_ROWS = 896
EDGE_ROWS = S + 8

vmem = pl.BlockSpec(memory_space=pltpu.VMEM)
hbm = pl.BlockSpec(memory_space=pltpu.HBM)


def row_offsets():
    offsets, at = [], 0
    for group in range(S // GROUP):
        offsets.append(at)
        at += GROUP * (S - GROUP * group)
    return offsets, at


OFFSETS, WEIGHT_ROWS = row_offsets()


def call(kernel, outs, in_specs, name, flops=0, nbytes=1 << 20, scratch=(), place=vmem):
    single = not isinstance(outs, (tuple, list))
    return pl.pallas_call(
        kernel,
        out_shape=outs,
        in_specs=in_specs,
        out_specs=place if single else [place] * len(outs),
        scratch_shapes=list(scratch),
        name=name,
        cost_estimate=pl.CostEstimate(flops=flops, bytes_accessed=nbytes, transcendentals=0),
        compiler_params=pltpu.CompilerParams(vmem_limit_bytes=32 << 20),
    )


def shape(*dims, dtype=f32):
    return jax.ShapeDtypeStruct(dims, dtype)


def swap_groups(tiles):
    group = lax.broadcasted_iota(jnp.int32, (8, Y), 1) // 8
    tiles = list(tiles)
    tiles = [tiles[-i % B] for i in range(B)]
    tiles = [pltpu.roll(tile, 8 * (-i % B), 1) if i else tile for i, tile in enumerate(tiles)]
    for bit in (1, 2, 4, 8):
        upper = (group & bit) != 0
        tiles = [jnp.where(upper, tiles[i - bit], tiles[i]) for i in range(B)]
    return [pltpu.roll(tile, Y - 8 * i, 1) if i else tile for i, tile in enumerate(tiles)]


def run_of(index):
    return jnp.where(lax.axis_index("gy") == 0, index, B - 1 - index)


def own_cells(rows, run):
    shift = lax.rem(Y - 8 * run, Y)
    moved = pltpu.roll(pltpu.roll(rows, shift, 1), 0, 1, stride=8, stride_axis=0)
    group = lax.broadcasted_iota(jnp.int32, (B, Y), 1) // 8
    row = lax.broadcasted_iota(jnp.int32, (B, Y), 0)
    return jnp.sum(jnp.where(group == row, moved, 0.0), axis=0, keepdims=True)


def pack_kernel(
    n_hbm, c_hbm, rate_hbm, vel_hbm, factor_hbm, diff_hbm, kernel_hbm, target_hbm,
    send_ref, own_ref, factor_ref, diff_ref, kernel_ref, target_ref,
    n_ref, c_ref, rate_ref, vel_ref, row_ref, sems,
):
    run = run_of(lax.axis_index("sec"))
    pairs = (
        (factor_hbm, row_ref.at[pl.ds(0, 1)]),
        (diff_hbm, row_ref.at[pl.ds(8, 1)]),
        (rate_hbm, rate_ref),
        (vel_hbm, vel_ref),
        (n_hbm, n_ref),
        (c_hbm, c_ref),
        (kernel_hbm, kernel_ref),
        (target_hbm, target_ref),
    )
    copies = [pltpu.make_async_copy(a, b, sems.at[i]) for i, (a, b) in enumerate(pairs)]
    for copy in copies:
        copy.start()
    for copy in copies[:4]:
        copy.wait()
    rows = [own_cells(rate_ref[pl.ds(h * 16, 16), :], run) for h in range(2)]
    rows += [own_cells(vel_ref[pl.ds(h * 16, 16), :], run) for h in range(4)]
    own_ref[...] = jnp.concatenate(rows + [jnp.zeros((2, Y), f32)], axis=0)
    factor_ref[...] = jnp.broadcast_to(row_ref[pl.ds(0, 1), :], (S, S)).T
    diff_ref[...] = jnp.broadcast_to(row_ref[pl.ds(8, 1), :], (S, S)).T
    for array, ref in enumerate((n_ref, c_ref)):
        copies[4 + array].wait()
        for half in range(2):
            tiles = swap_groups(
                ref[pl.ds(half * 16 + g, R, stride=L * X), :] for g in range(B)
            )
            for d, tile in enumerate(tiles):
                at = pl.multiple_of(run_of(d) * 32 + array * 16 + half * 8, 8)
                send_ref[pl.ds(at, 8), :] = tile
    for copy in copies[6:]:
        copy.wait()


def lane_parts():
    lane = lax.broadcasted_iota(jnp.int32, (8, Y), 1)
    return lane // 64, (lane // 8) % 8, lane % 8


def turn(tile, shift):
    shift = shift % Y
    return tile if shift == 0 else pltpu.roll(tile, shift, 1)


def even_places():
    return lax.rem(lax.axis_index("gx"), 2) == 0, lax.rem(run_of(lax.axis_index("sec")), 2) == 0


def pack_edges(tiles, which, even, refs, rows):
    _, x, y = which
    x_up, x_down, y_up, y_down = (jnp.zeros((8, Y), f32) for _ in range(4))
    for i, tile in enumerate(tiles):
        x_up = jnp.where(x == i, turn(tile, 8 * (i - 7)), x_up)
        x_down = jnp.where(x == 7 - i, turn(tile, 8 * (7 - i)), x_down)
        y_up = jnp.where(y == i, turn(tile, i - 7), y_up)
        y_down = jnp.where(y == 7 - i, turn(tile, 7 - i), y_down)
    for i, (up, down) in enumerate(((x_up, x_down), (y_up, y_down))):
        refs[2 * i][rows, :] = jnp.where(even[i], up, down)
        refs[2 * i + 1][rows, :] = jnp.where(even[i], down, up)


def received_edges(even, refs, rows):
    edges = []
    for i in range(2):
        a, b = (ref[rows, :] for ref in refs[2 * i : 2 * i + 2])
        edges += [jnp.where(even[i], b, a), jnp.where(even[i], a, b)]
    return edges


def shifted(tile, edges, i, which):
    _, x, y = which
    from_low_x, from_high_x, from_low_y, from_high_y = edges
    x_minus = jnp.where(x == 0, turn(from_low_x, -8 * i), turn(tile, 8))
    x_plus = jnp.where(x == 7, turn(from_high_x, 8 * i), turn(tile, -8))
    y_minus = jnp.where(y == 0, turn(from_low_y, -i), turn(tile, 1))
    y_plus = jnp.where(y == 7, turn(from_high_y, i), turn(tile, -1))
    return x_plus, x_minus, y_plus, y_minus


def vertical(low, high, which):
    first = which[0] == 0
    a, b = turn(low, 64), turn(high, 64)
    return (
        a + jnp.where(first, low, b) - 2.0 * low,
        b + jnp.where(first, a, high) - 2.0 * high,
    )


def adjoint_kernel(
    got_ref, own_ref, factor_ref, adj_ref, coef_ref, x_first_ref, x_second_ref, y_first_ref, y_second_ref
):
    block = lax.broadcasted_iota(jnp.int32, (B, Y), 0)
    for h in range(2):
        rate = own_ref[pl.ds(h, 1), :]
        growths, inverses = [], []
        for i in range(R):
            growth = step_size * (rate * factor_ref[pl.ds(i, B, stride=R), :])
            inverse = 1.0 / (1.0 + growth)
            coef_ref[pl.ds(INV + (i * 2 + h) * B, B), :] = inverse
            growths.append(growth)
            inverses.append(inverse)
        product = None
        for i in range(R):
            prior = growths[i - 1] if i else jnp.where(block == 0, 0.0, pltpu.roll(growths[R - 1], 1, 0))
            ratio = prior * inverses[i]
            product = ratio if product is None else ratio * product
            coef_ref[pl.ds(FWD + (i * 2 + h) * B, B), :] = ratio
            coef_ref[pl.ds(FWD_PI + (i * 2 + h) * B, B), :] = product
        q = jnp.where(block == 0, 0.0, product)
        for turns, hop in enumerate((1, 2, 4, 8)):
            coef_ref[pl.ds(FWD_Q + (turns * 2 + h) * B, B), :] = q
            q = q * pltpu.roll(q, hop, 0)
        value, product, values = None, None, []
        for i in reversed(range(R)):
            source = got_ref[pl.ds(16 + h * 8 + i, B, stride=32), :] * inverses[i]
            ratio = growths[i] * inverses[i]
            value = source if value is None else source + ratio * value
            product = ratio if product is None else ratio * product
            values.append((i, value, product))
        q = jnp.where(block == B - 1, 0.0, product)
        for hop in (1, 2, 4, 8):
            value = value + q * pltpu.roll(value, B - hop, 0)
            q = q * pltpu.roll(q, B - hop, 0)
        carry = jnp.where(block == B - 1, 0.0, pltpu.roll(value, B - 1, 0))
        for i, local, product in values:
            adj_ref[pl.ds(h * S + i, B, stride=R), :] = local + product * carry
    which = lane_parts()
    even = even_places()
    refs = (x_first_ref, x_second_ref, y_first_ref, y_second_ref)
    for b in range(B):
        tiles = [got_ref[pl.ds(b * 32 + h * 8, 8), :] for h in range(2)]
        tiles += [adj_ref[pl.ds(h * S + b * 8, 8), :] for h in range(2)]
        pack_edges(tiles, which, even, refs, pl.ds(b * 8, 8))
    winds = [jnp.broadcast_to(own_ref[pl.ds(2 + h, 1), :], (8, Y)) for h in range(4)]
    pack_edges(winds, which, even, refs, pl.ds(S, 8))


def split(value):
    high = value.astype(bf16)
    return high, (value - high.astype(f32)).astype(bf16)


def three(value):
    high, rest = split(value)
    return jnp.concatenate([high, rest, high], axis=1)


def pair_kernel(
    got_ref, adj_ref, kernel_ref, target_ref, gain_out, coag_out,
    n_ref, a_ref, gain_ref, part_ref, weight_ref, rows_ref,
):
    kernel = kernel_ref[...]
    target = target_ref[...].astype(f32)
    turned = kernel.T
    target_turned = target.T
    same = target == target_turned
    one = 0.5 * kernel + jnp.where(same, 0.5 * turned, 0.0)
    two = jnp.where(same, 0.0, 0.5 * turned)
    for i, part in enumerate((target, target_turned, one, two)):
        rows_ref[pl.ds(i * S, S), :] = part

    for group in range(S // GROUP):
        low = group * GROUP
        count = S - low
        ids = (lax.broadcasted_iota(jnp.int32, (count, S), 0) + low).astype(f32)

        def build(k, _, low=low, count=count, ids=ids, start=OFFSETS[group]):
            t1, t2, one, two = (rows_ref[pl.ds(i * S + low + k, 1), :] for i in range(4))
            high, rest = split(jnp.where(ids == t1, one, jnp.where(ids == t2, two, 0.0)))
            rows = pl.ds(pl.multiple_of(start + k * count, 16), count)
            weight_ref[rows, :] = jnp.concatenate([high, rest], axis=1)
            return 0

        lax.fori_loop(0, GROUP, build, 0, unroll=True)

    for r in range(2):
        for b in range(B):
            n_ref[pl.ds(b * 8, 8), pl.ds(r * Y, Y)] = got_ref[pl.ds(b * 32 + r * 8, 8), :]
        a_ref[:, pl.ds(r * Y, Y)] = adj_ref[pl.ds(r * S, S), :]
    number = n_ref[...]
    high, rest = split(number)
    right = jnp.concatenate([high, high, rest], axis=0)
    gain_ref[...] = jnp.zeros_like(gain_ref)

    for group in range(S // GROUP):
        low = group * GROUP
        count = S - low

        left = weight_ref[pl.ds(OFFSETS[group], GROUP * count), :]
        left = jnp.concatenate([left, left[:, :S]], axis=1)
        found = jnp.dot(left, right, preferred_element_type=f32).reshape(GROUP, count, 2 * Y)
        total = gain_ref[pl.ds(low, count), :]
        adjoint = a_ref[pl.ds(low, count), :]
        for p in range(GROUP):
            k = low + p
            total = total + found[p] * n_ref[pl.ds(k, 1), :]
            share = (found[p] * adjoint).reshape(count // 8, 8, 2 * Y).sum(axis=0)
            for r in range(2):
                part_ref[pl.ds(r * 8 * S + k * 8, 8), :] = share[:, r * Y : (r + 1) * Y]
        gain_ref[pl.ds(low, count), :] = total

    adjoint = a_ref[...]
    pull = jnp.dot(three(kernel), right, preferred_element_type=f32)
    high, rest = split(adjoint * number)
    right = jnp.concatenate([high, high, rest], axis=0)
    back = jnp.dot(three(turned), right, preferred_element_type=f32)
    gain = step_size * (0.5 * gain_ref[...] - number * pull)
    for r in range(2):
        gain_out[pl.ds(r * S, S), :] = gain[:, r * Y : (r + 1) * Y]
    other = adjoint * pull + back
    for r in range(2):
        coag = part_ref[pl.ds(r * 8 * S, S, stride=8), :]
        for j in range(1, 8):
            coag = coag + part_ref[pl.ds(r * 8 * S + j, S, stride=8), :]
        coag_out[pl.ds(r * S, S), :] = coag - other[:, r * Y : (r + 1) * Y]


def next_kernel(
    got_ref, adj_ref, own_ref, diff_ref, coef_ref, gain_ref, coag_ref,
    x_first_ref, x_second_ref, y_first_ref, y_second_ref, send_ref, right_ref,
):
    which = lane_parts()
    even = even_places()
    refs = (x_first_ref, x_second_ref, y_first_ref, y_second_ref)
    wind_edges = received_edges(even, refs, pl.ds(S, 8))
    winds = []
    for h in range(2):
        u = jnp.broadcast_to(own_ref[pl.ds(2 + h, 1), :], (8, Y))
        w = jnp.broadcast_to(own_ref[pl.ds(4 + h, 1), :], (8, Y))
        up, um, _, _ = shifted(u, wind_edges, h, which)
        _, _, wp, wm = shifted(w, wind_edges, 2 + h, which)
        winds.append((0.5 * u, 0.5 * w, 0.5 * up, 0.5 * um, 0.5 * wp, 0.5 * wm))
    for b in range(B):
        edges = received_edges(even, refs, pl.ds(b * 8, 8))
        diffusion = diff_ref[pl.ds(b * 8, 8), :]
        numbers = [got_ref[pl.ds(b * 32 + h * 8, 8), :] for h in range(2)]
        adjoints = [adj_ref[pl.ds(h * S + b * 8, 8), :] for h in range(2)]
        number_levels = vertical(*numbers, which)
        adjoint_levels = vertical(*adjoints, which)
        for h in range(2):
            u, w, up, um, wp, wm = winds[h]
            rows = pl.ds(h * S + b * 8, 8)
            v = numbers[h]
            xp, xm, yp, ym = shifted(v, edges, h, which)
            moved = (
                diffusion * (xp + xm + yp + ym - 4.0 * v)
                - u * (xp - xm)
                - w * (yp - ym)
                + vertical_mix * number_levels[h]
            )
            right_ref[rows, :] = v + step_size * moved + gain_ref[rows, :]
            v = adjoints[h]
            xp, xm, yp, ym = shifted(v, edges, 2 + h, which)
            moved = (
                diffusion * (xp + xm + yp + ym - 4.0 * v)
                + (up * xp - um * xm)
                + (wp * yp - wm * ym)
                + vertical_mix * adjoint_levels[h]
            )
            send_ref[pl.ds(b * 32 + 16 + h * 8, 8), :] = v + step_size * (moved + coag_ref[rows, :])
    block = lax.broadcasted_iota(jnp.int32, (B, Y), 0)
    for h in range(2):
        value, values = None, []
        for i in range(R):
            at = (i * 2 + h) * B
            source = right_ref[pl.ds(h * S + i, B, stride=R), :] * coef_ref[pl.ds(INV + at, B), :]
            value = source if value is None else source + coef_ref[pl.ds(FWD + at, B), :] * value
            values.append(value)
        for turns, hop in enumerate((1, 2, 4, 8)):
            q = coef_ref[pl.ds(FWD_Q + (turns * 2 + h) * B, B), :]
            value = value + q * pltpu.roll(value, hop, 0)
        carry = jnp.where(block == 0, 0.0, pltpu.roll(value, 1, 0))
        for i in range(R):
            full = values[i] + coef_ref[pl.ds(FWD_PI + (i * 2 + h) * B, B), :] * carry
            send_ref[pl.ds(h * 8 + i, B, stride=32), :] = full


def unpack_kernel(back_ref, next_hbm, gradient_hbm, next_ref, gradient_ref, sems):
    copies = []
    for array, (ref, out) in enumerate(((next_ref, next_hbm), (gradient_ref, gradient_hbm))):
        for half in range(2):
            tiles = swap_groups(
                back_ref[pl.ds(pl.multiple_of(run_of(d) * 32 + array * 16 + half * 8, 8), 8), :]
                for d in range(B)
            )
            for g, tile in enumerate(tiles):
                ref[pl.ds(half * 16 + g, R, stride=L * X), :] = tile
        copies.append(pltpu.make_async_copy(ref, out, sems.at[array]))
        copies[-1].start()
    for copy in copies:
        copy.wait()


def exchange(rows):
    count = rows.shape[0]
    parts = lax.all_to_all(
        rows.reshape(B, count // B, Y), "sec", split_axis=0, concat_axis=0, tiled=True
    )
    return parts.reshape(count, Y)


def swaps(count, first, place=lambda i: i):
    pairs = [(place(i), place((i + 1) % count)) for i in range(first, count, 2)]
    return pairs + [(b, a) for a, b in pairs]


def y_place(position):
    half, run = position // B, position % B
    return (B - 1 - run if half else run) * 2 + half


def per_device(
    number, cotangent, growth_rate, section_factor, velocity, diffusivity, kernel, target
):
    send, own, factor, diff, kernel_in, target_in = call(
        pack_kernel,
        (
            shape(512, Y), shape(8, Y), shape(S, S), shape(S, S), shape(S, S),
            shape(S, S, dtype=jnp.int32),
        ),
        [hbm] * 8,
        "pack",
        scratch=(
            pltpu.VMEM((256, Y), f32),
            pltpu.VMEM((256, Y), f32),
            pltpu.VMEM((32, Y), f32),
            pltpu.VMEM((64, Y), f32),
            pltpu.VMEM((16, Y), f32),
            pltpu.SemaphoreType.DMA((8,)),
        ),
    )(
        *(
            pltpu.with_memory_space_constraint(array, pltpu.HBM)
            for array in (
                number.reshape(256, Y),
                cotangent.reshape(256, Y),
                growth_rate.reshape(32, Y),
                velocity.reshape(64, Y),
                section_factor.reshape(1, S),
                diffusivity.reshape(1, S),
                kernel,
                target,
            )
        )
    )
    got = exchange(send)
    adj, coef, x_first, x_second, y_first, y_second = call(
        adjoint_kernel,
        (shape(256, Y), shape(COEF_ROWS, Y)) + (shape(EDGE_ROWS, Y),) * 4,
        [vmem] * 3,
        "adjoint",
    )(got, own, factor)
    x_count = lax.axis_size("gx")
    edges = (
        lax.ppermute(x_first, "gx", swaps(x_count, 0)),
        lax.ppermute(x_second, "gx", swaps(x_count, 1)),
        lax.ppermute(y_first, ("sec", "gy"), swaps(2 * B, 0, y_place)),
        lax.ppermute(y_second, ("sec", "gy"), swaps(2 * B, 1, y_place)),
    )
    gain, coag = call(
        pair_kernel,
        (shape(256, Y), shape(256, Y)),
        [vmem] * 4,
        "pairs",
        flops=1 << 32,
        nbytes=8 << 20,
        scratch=(
            pltpu.VMEM((S, 2 * Y), f32),
            pltpu.VMEM((S, 2 * Y), f32),
            pltpu.VMEM((S, 2 * Y), f32),
            pltpu.VMEM((2 * S * 8, Y), f32),
            pltpu.VMEM((WEIGHT_ROWS, 2 * S), bf16),
            pltpu.VMEM((4 * S, S), f32),
        ),
    )(got, adj, kernel_in, target_in)
    send_back = call(
        next_kernel, shape(512, Y), [vmem] * 11, "next", scratch=(pltpu.VMEM((256, Y), f32),)
    )(got, adj, own, diff, coef, gain, coag, *edges)
    next_rows, gradient = call(
        unpack_kernel,
        (shape(256, Y), shape(256, Y)),
        [vmem],
        "unpack",
        scratch=(
            pltpu.VMEM((256, Y), f32),
            pltpu.VMEM((256, Y), f32),
            pltpu.SemaphoreType.DMA((2,)),
        ),
        place=hbm,
    )(exchange(send_back))
    return next_rows.reshape(number.shape), gradient.reshape(number.shape)


def solution(mesh):
    return jax.shard_map(
        per_device,
        mesh=mesh,
        in_specs=(
            P("sec", None, "gx", "gy"),
            P("sec", None, "gx", "gy"),
            P(None, "gx", "gy"),
            P(),
            P(None, None, "gx", "gy"),
            P(),
            P(),
            P(),
        ),
        out_specs=(P("sec", None, "gx", "gy"), P("sec", None, "gx", "gy")),
        check_vma=False,
    )
```

```python
import jax
import jax.numpy as jnp
from jax import lax
from jax.experimental import pallas as pl
from jax.experimental.pallas import tpu as pltpu
from jax.sharding import PartitionSpec as P

step_size = 0.25
vertical_mix = 0.2
highest = lax.Precision.HIGHEST
f32 = jnp.float32
bf16 = jnp.bfloat16

S = 128
B = 16
R = 8
L = 4
X = 8
Y = 128
GROUP = 16

INV, FWD, FWD_PI = (256 * i for i in range(3))
FWD_Q = 768
COEF_ROWS = 896
EDGE_ROWS = S + 8

vmem = pl.BlockSpec(memory_space=pltpu.VMEM)
hbm = pl.BlockSpec(memory_space=pltpu.HBM)


def row_offsets():
    offsets, at = [], 0
    for group in range(S // GROUP):
        offsets.append(at)
        at += GROUP * (S - GROUP * group)
    return offsets, at


OFFSETS, WEIGHT_ROWS = row_offsets()


def call(kernel, outs, in_specs, name, flops=0, nbytes=1 << 20, scratch=(), place=vmem):
    single = not isinstance(outs, (tuple, list))
    return pl.pallas_call(
        kernel,
        out_shape=outs,
        in_specs=in_specs,
        out_specs=place if single else [place] * len(outs),
        scratch_shapes=list(scratch),
        name=name,
        cost_estimate=pl.CostEstimate(flops=flops, bytes_accessed=nbytes, transcendentals=0),
        compiler_params=pltpu.CompilerParams(vmem_limit_bytes=32 << 20),
    )


def shape(*dims, dtype=f32):
    return jax.ShapeDtypeStruct(dims, dtype)


def swap_groups(tiles):
    group = lax.broadcasted_iota(jnp.int32, (8, Y), 1) // 8
    tiles = list(tiles)
    tiles = [tiles[-i % B] for i in range(B)]
    tiles = [pltpu.roll(tile, 8 * (-i % B), 1) if i else tile for i, tile in enumerate(tiles)]
    for bit in (1, 2, 4, 8):
        upper = (group & bit) != 0
        tiles = [jnp.where(upper, tiles[i - bit], tiles[i]) for i in range(B)]
    return [pltpu.roll(tile, Y - 8 * i, 1) if i else tile for i, tile in enumerate(tiles)]


def run_of(index):
    return jnp.where(lax.axis_index("gy") == 0, index, B - 1 - index)


def own_cells(rows, run):
    shift = lax.rem(Y - 8 * run, Y)
    moved = pltpu.roll(pltpu.roll(rows, shift, 1), 0, 1, stride=8, stride_axis=0)
    group = lax.broadcasted_iota(jnp.int32, (B, Y), 1) // 8
    row = lax.broadcasted_iota(jnp.int32, (B, Y), 0)
    return jnp.sum(jnp.where(group == row, moved, 0.0), axis=0, keepdims=True)


def pack_kernel(
    n_hbm, c_hbm, rate_hbm, vel_hbm, factor_hbm, diff_hbm, kernel_hbm, target_hbm,
    send_ref, own_ref, factor_ref, diff_ref, kernel_ref, target_ref,
    n_ref, c_ref, rate_ref, vel_ref, row_ref, sems,
):
    run = run_of(lax.axis_index("sec"))
    pairs = (
        (factor_hbm, row_ref.at[pl.ds(0, 1)]),
        (diff_hbm, row_ref.at[pl.ds(8, 1)]),
        (rate_hbm, rate_ref),
        (vel_hbm, vel_ref),
        (n_hbm, n_ref),
        (c_hbm, c_ref),
        (kernel_hbm, kernel_ref),
        (target_hbm, target_ref),
    )
    copies = [pltpu.make_async_copy(a, b, sems.at[i]) for i, (a, b) in enumerate(pairs)]
    for copy in copies:
        copy.start()
    for copy in copies[:4]:
        copy.wait()
    rows = [own_cells(rate_ref[pl.ds(h * 16, 16), :], run) for h in range(2)]
    rows += [own_cells(vel_ref[pl.ds(h * 16, 16), :], run) for h in range(4)]
    own_ref[...] = jnp.concatenate(rows + [jnp.zeros((2, Y), f32)], axis=0)
    factor_ref[...] = jnp.broadcast_to(row_ref[pl.ds(0, 1), :], (S, S)).T
    diff_ref[...] = jnp.broadcast_to(row_ref[pl.ds(8, 1), :], (S, S)).T
    for array, ref in enumerate((n_ref, c_ref)):
        copies[4 + array].wait()
        for half in range(2):
            tiles = swap_groups(
                ref[pl.ds(half * 16 + g, R, stride=L * X), :] for g in range(B)
            )
            for d, tile in enumerate(tiles):
                at = pl.multiple_of(run_of(d) * 32 + array * 16 + half * 8, 8)
                send_ref[pl.ds(at, 8), :] = tile
    for copy in copies[6:]:
        copy.wait()


def lane_parts():
    lane = lax.broadcasted_iota(jnp.int32, (8, Y), 1)
    return lane // 64, (lane // 8) % 8, lane % 8


def turn(tile, shift):
    shift = shift % Y
    return tile if shift == 0 else pltpu.roll(tile, shift, 1)


def even_places():
    return lax.rem(lax.axis_index("gx"), 2) == 0, lax.rem(run_of(lax.axis_index("sec")), 2) == 0


def pack_edges(tiles, which, even, refs, rows):
    _, x, y = which
    x_up, x_down, y_up, y_down = (jnp.zeros((8, Y), f32) for _ in range(4))
    for i, tile in enumerate(tiles):
        x_up = jnp.where(x == i, turn(tile, 8 * (i - 7)), x_up)
        x_down = jnp.where(x == 7 - i, turn(tile, 8 * (7 - i)), x_down)
        y_up = jnp.where(y == i, turn(tile, i - 7), y_up)
        y_down = jnp.where(y == 7 - i, turn(tile, 7 - i), y_down)
    for i, (up, down) in enumerate(((x_up, x_down), (y_up, y_down))):
        refs[2 * i][rows, :] = jnp.where(even[i], up, down)
        refs[2 * i + 1][rows, :] = jnp.where(even[i], down, up)


def received_edges(even, refs, rows):
    edges = []
    for i in range(2):
        a, b = (ref[rows, :] for ref in refs[2 * i : 2 * i + 2])
        edges += [jnp.where(even[i], b, a), jnp.where(even[i], a, b)]
    return edges


def shifted(tile, edges, i, which):
    _, x, y = which
    from_low_x, from_high_x, from_low_y, from_high_y = edges
    x_minus = jnp.where(x == 0, turn(from_low_x, -8 * i), turn(tile, 8))
    x_plus = jnp.where(x == 7, turn(from_high_x, 8 * i), turn(tile, -8))
    y_minus = jnp.where(y == 0, turn(from_low_y, -i), turn(tile, 1))
    y_plus = jnp.where(y == 7, turn(from_high_y, i), turn(tile, -1))
    return x_plus, x_minus, y_plus, y_minus


def vertical(low, high, which):
    first = which[0] == 0
    a, b = turn(low, 64), turn(high, 64)
    return (
        a + jnp.where(first, low, b) - 2.0 * low,
        b + jnp.where(first, a, high) - 2.0 * high,
    )


def adjoint_kernel(
    got_ref, own_ref, factor_ref, adj_ref, coef_ref, x_first_ref, x_second_ref, y_first_ref, y_second_ref
):
    block = lax.broadcasted_iota(jnp.int32, (B, Y), 0)
    for h in range(2):
        rate = own_ref[pl.ds(h, 1), :]
        growths, inverses = [], []
        for i in range(R):
            growth = step_size * (rate * factor_ref[pl.ds(i, B, stride=R), :])
            inverse = 1.0 / (1.0 + growth)
            coef_ref[pl.ds(INV + (i * 2 + h) * B, B), :] = inverse
            growths.append(growth)
            inverses.append(inverse)
        product = None
        for i in range(R):
            prior = growths[i - 1] if i else jnp.where(block == 0, 0.0, pltpu.roll(growths[R - 1], 1, 0))
            ratio = prior * inverses[i]
            product = ratio if product is None else ratio * product
            coef_ref[pl.ds(FWD + (i * 2 + h) * B, B), :] = ratio
            coef_ref[pl.ds(FWD_PI + (i * 2 + h) * B, B), :] = product
        q = jnp.where(block == 0, 0.0, product)
        for turns, hop in enumerate((1, 2, 4, 8)):
            coef_ref[pl.ds(FWD_Q + (turns * 2 + h) * B, B), :] = q
            q = q * pltpu.roll(q, hop, 0)
        value, product, values = None, None, []
        for i in reversed(range(R)):
            source = got_ref[pl.ds(16 + h * 8 + i, B, stride=32), :] * inverses[i]
            ratio = growths[i] * inverses[i]
            value = source if value is None else source + ratio * value
            product = ratio if product is None else ratio * product
            values.append((i, value, product))
        q = jnp.where(block == B - 1, 0.0, product)
        for hop in (1, 2, 4, 8):
            value = value + q * pltpu.roll(value, B - hop, 0)
            q = q * pltpu.roll(q, B - hop, 0)
        carry = jnp.where(block == B - 1, 0.0, pltpu.roll(value, B - 1, 0))
        for i, local, product in values:
            adj_ref[pl.ds(h * S + i, B, stride=R), :] = local + product * carry
    which = lane_parts()
    even = even_places()
    refs = (x_first_ref, x_second_ref, y_first_ref, y_second_ref)
    for b in range(B):
        tiles = [got_ref[pl.ds(b * 32 + h * 8, 8), :] for h in range(2)]
        tiles += [adj_ref[pl.ds(h * S + b * 8, 8), :] for h in range(2)]
        pack_edges(tiles, which, even, refs, pl.ds(b * 8, 8))
    winds = [jnp.broadcast_to(own_ref[pl.ds(2 + h, 1), :], (8, Y)) for h in range(4)]
    pack_edges(winds, which, even, refs, pl.ds(S, 8))


def split(value):
    high = value.astype(bf16)
    return high, (value - high.astype(f32)).astype(bf16)


def pair_kernel(
    got_ref, adj_ref, kernel_ref, target_ref, gain_out, coag_out,
    n_ref, a_ref, gain_ref, part_ref, weight_ref, rows_ref,
):
    kernel = kernel_ref[...]
    target = target_ref[...].astype(f32)
    turned = kernel.T
    target_turned = target.T
    same = target == target_turned
    one = 0.5 * kernel + jnp.where(same, 0.5 * turned, 0.0)
    two = jnp.where(same, 0.0, 0.5 * turned)
    for i, part in enumerate((target, target_turned, one, two)):
        rows_ref[pl.ds(i * S, S), :] = part

    for group in range(S // GROUP):
        low = group * GROUP
        count = S - low
        ids = (lax.broadcasted_iota(jnp.int32, (count, S), 0) + low).astype(f32)

        def build(k, _, low=low, count=count, ids=ids, start=OFFSETS[group]):
            t1, t2, one, two = (rows_ref[pl.ds(i * S + low + k, 1), :] for i in range(4))
            high, rest = split(jnp.where(ids == t1, one, jnp.where(ids == t2, two, 0.0)))
            rows = pl.ds(pl.multiple_of(start + k * count, 16), count)
            weight_ref[rows, :] = jnp.concatenate([high, rest], axis=1)
            return 0

        lax.fori_loop(0, GROUP, build, 0, unroll=True)

    for r in range(2):
        for b in range(B):
            n_ref[pl.ds(b * 8, 8), pl.ds(r * Y, Y)] = got_ref[pl.ds(b * 32 + r * 8, 8), :]
        a_ref[:, pl.ds(r * Y, Y)] = adj_ref[pl.ds(r * S, S), :]
    number = n_ref[...]
    high, rest = split(number)
    right = jnp.concatenate([high, high, rest], axis=0)
    gain_ref[...] = jnp.zeros_like(gain_ref)

    for group in range(S // GROUP):
        low = group * GROUP
        count = S - low

        left = weight_ref[pl.ds(OFFSETS[group], GROUP * count), :]
        left = jnp.concatenate([left, left[:, :S]], axis=1)
        found = jnp.dot(left, right, preferred_element_type=f32).reshape(GROUP, count, 2 * Y)
        total = gain_ref[pl.ds(low, count), :]
        adjoint = a_ref[pl.ds(low, count), :]
        for p in range(GROUP):
            k = low + p
            total = total + found[p] * n_ref[pl.ds(k, 1), :]
            share = (found[p] * adjoint).reshape(count // 8, 8, 2 * Y).sum(axis=0)
            for r in range(2):
                part_ref[pl.ds(r * 8 * S + k * 8, 8), :] = share[:, r * Y : (r + 1) * Y]
        gain_ref[pl.ds(low, count), :] = total

    adjoint = a_ref[...]
    pull = jnp.dot(kernel, number, precision=highest, preferred_element_type=f32)
    back = jnp.dot(turned, adjoint * number, precision=highest, preferred_element_type=f32)
    gain = step_size * (0.5 * gain_ref[...] - number * pull)
    for r in range(2):
        gain_out[pl.ds(r * S, S), :] = gain[:, r * Y : (r + 1) * Y]
    other = adjoint * pull + back
    for r in range(2):
        coag = part_ref[pl.ds(r * 8 * S, S, stride=8), :]
        for j in range(1, 8):
            coag = coag + part_ref[pl.ds(r * 8 * S + j, S, stride=8), :]
        coag_out[pl.ds(r * S, S), :] = coag - other[:, r * Y : (r + 1) * Y]


def next_kernel(
    got_ref, adj_ref, own_ref, diff_ref, coef_ref, gain_ref, coag_ref,
    x_first_ref, x_second_ref, y_first_ref, y_second_ref, send_ref, right_ref,
):
    which = lane_parts()
    even = even_places()
    refs = (x_first_ref, x_second_ref, y_first_ref, y_second_ref)
    wind_edges = received_edges(even, refs, pl.ds(S, 8))
    winds = []
    for h in range(2):
        u = jnp.broadcast_to(own_ref[pl.ds(2 + h, 1), :], (8, Y))
        w = jnp.broadcast_to(own_ref[pl.ds(4 + h, 1), :], (8, Y))
        up, um, _, _ = shifted(u, wind_edges, h, which)
        _, _, wp, wm = shifted(w, wind_edges, 2 + h, which)
        winds.append((0.5 * u, 0.5 * w, 0.5 * up, 0.5 * um, 0.5 * wp, 0.5 * wm))
    for b in range(B):
        edges = received_edges(even, refs, pl.ds(b * 8, 8))
        diffusion = diff_ref[pl.ds(b * 8, 8), :]
        numbers = [got_ref[pl.ds(b * 32 + h * 8, 8), :] for h in range(2)]
        adjoints = [adj_ref[pl.ds(h * S + b * 8, 8), :] for h in range(2)]
        number_levels = vertical(*numbers, which)
        adjoint_levels = vertical(*adjoints, which)
        for h in range(2):
            u, w, up, um, wp, wm = winds[h]
            rows = pl.ds(h * S + b * 8, 8)
            v = numbers[h]
            xp, xm, yp, ym = shifted(v, edges, h, which)
            moved = (
                diffusion * (xp + xm + yp + ym - 4.0 * v)
                - u * (xp - xm)
                - w * (yp - ym)
                + vertical_mix * number_levels[h]
            )
            right_ref[rows, :] = v + step_size * moved + gain_ref[rows, :]
            v = adjoints[h]
            xp, xm, yp, ym = shifted(v, edges, 2 + h, which)
            moved = (
                diffusion * (xp + xm + yp + ym - 4.0 * v)
                + (up * xp - um * xm)
                + (wp * yp - wm * ym)
                + vertical_mix * adjoint_levels[h]
            )
            send_ref[pl.ds(b * 32 + 16 + h * 8, 8), :] = v + step_size * (moved + coag_ref[rows, :])
    block = lax.broadcasted_iota(jnp.int32, (B, Y), 0)
    for h in range(2):
        value, values = None, []
        for i in range(R):
            at = (i * 2 + h) * B
            source = right_ref[pl.ds(h * S + i, B, stride=R), :] * coef_ref[pl.ds(INV + at, B), :]
            value = source if value is None else source + coef_ref[pl.ds(FWD + at, B), :] * value
            values.append(value)
        for turns, hop in enumerate((1, 2, 4, 8)):
            q = coef_ref[pl.ds(FWD_Q + (turns * 2 + h) * B, B), :]
            value = value + q * pltpu.roll(value, hop, 0)
        carry = jnp.where(block == 0, 0.0, pltpu.roll(value, 1, 0))
        for i in range(R):
            full = values[i] + coef_ref[pl.ds(FWD_PI + (i * 2 + h) * B, B), :] * carry
            send_ref[pl.ds(h * 8 + i, B, stride=32), :] = full


def unpack_kernel(back_ref, next_hbm, gradient_hbm, next_ref, gradient_ref, sems):
    copies = []
    for array, (ref, out) in enumerate(((next_ref, next_hbm), (gradient_ref, gradient_hbm))):
        for half in range(2):
            tiles = swap_groups(
                back_ref[pl.ds(pl.multiple_of(run_of(d) * 32 + array * 16 + half * 8, 8), 8), :]
                for d in range(B)
            )
            for g, tile in enumerate(tiles):
                ref[pl.ds(half * 16 + g, R, stride=L * X), :] = tile
        copies.append(pltpu.make_async_copy(ref, out, sems.at[array]))
        copies[-1].start()
    for copy in copies:
        copy.wait()


def exchange(rows):
    count = rows.shape[0]
    parts = lax.all_to_all(
        rows.reshape(B, count // B, Y), "sec", split_axis=0, concat_axis=0, tiled=True
    )
    return parts.reshape(count, Y)


def swaps(count, first, place=lambda i: i):
    pairs = [(place(i), place((i + 1) % count)) for i in range(first, count, 2)]
    return pairs + [(b, a) for a, b in pairs]


def y_place(position):
    half, run = position // B, position % B
    return (B - 1 - run if half else run) * 2 + half


def per_device(
    number, cotangent, growth_rate, section_factor, velocity, diffusivity, kernel, target
):
    send, own, factor, diff, kernel_in, target_in = call(
        pack_kernel,
        (
            shape(512, Y), shape(8, Y), shape(S, S), shape(S, S), shape(S, S),
            shape(S, S, dtype=jnp.int32),
        ),
        [hbm] * 8,
        "pack",
        scratch=(
            pltpu.VMEM((256, Y), f32),
            pltpu.VMEM((256, Y), f32),
            pltpu.VMEM((32, Y), f32),
            pltpu.VMEM((64, Y), f32),
            pltpu.VMEM((16, Y), f32),
            pltpu.SemaphoreType.DMA((8,)),
        ),
    )(
        *(
            pltpu.with_memory_space_constraint(array, pltpu.HBM)
            for array in (
                number.reshape(256, Y),
                cotangent.reshape(256, Y),
                growth_rate.reshape(32, Y),
                velocity.reshape(64, Y),
                section_factor.reshape(1, S),
                diffusivity.reshape(1, S),
                kernel,
                target,
            )
        )
    )
    got = exchange(send)
    adj, coef, x_first, x_second, y_first, y_second = call(
        adjoint_kernel,
        (shape(256, Y), shape(COEF_ROWS, Y)) + (shape(EDGE_ROWS, Y),) * 4,
        [vmem] * 3,
        "adjoint",
    )(got, own, factor)
    x_count = lax.axis_size("gx")
    edges = (
        lax.ppermute(x_first, "gx", swaps(x_count, 0)),
        lax.ppermute(x_second, "gx", swaps(x_count, 1)),
        lax.ppermute(y_first, ("sec", "gy"), swaps(2 * B, 0, y_place)),
        lax.ppermute(y_second, ("sec", "gy"), swaps(2 * B, 1, y_place)),
    )
    gain, coag = call(
        pair_kernel,
        (shape(256, Y), shape(256, Y)),
        [vmem] * 4,
        "pairs",
        flops=1 << 32,
        nbytes=8 << 20,
        scratch=(
            pltpu.VMEM((S, 2 * Y), f32),
            pltpu.VMEM((S, 2 * Y), f32),
            pltpu.VMEM((S, 2 * Y), f32),
            pltpu.VMEM((2 * S * 8, Y), f32),
            pltpu.VMEM((WEIGHT_ROWS, 2 * S), bf16),
            pltpu.VMEM((4 * S, S), f32),
        ),
    )(got, adj, kernel_in, target_in)
    send_back = call(
        next_kernel, shape(512, Y), [vmem] * 11, "next", scratch=(pltpu.VMEM((256, Y), f32),)
    )(got, adj, own, diff, coef, gain, coag, *edges)
    next_rows, gradient = call(
        unpack_kernel,
        (shape(256, Y), shape(256, Y)),
        [vmem],
        "unpack",
        scratch=(
            pltpu.VMEM((256, Y), f32),
            pltpu.VMEM((256, Y), f32),
            pltpu.SemaphoreType.DMA((2,)),
        ),
        place=hbm,
    )(exchange(send_back))
    return next_rows.reshape(number.shape), gradient.reshape(number.shape)


def solution(mesh):
    return jax.shard_map(
        per_device,
        mesh=mesh,
        in_specs=(
            P("sec", None, "gx", "gy"),
            P("sec", None, "gx", "gy"),
            P(None, "gx", "gy"),
            P(),
            P(None, None, "gx", "gy"),
            P(),
            P(),
            P(),
        ),
        out_specs=(P("sec", None, "gx", "gy"), P("sec", None, "gx", "gy")),
        check_vma=False,
    )
```

```python
import jax
import jax.numpy as jnp
from jax import lax
from jax.experimental import pallas as pl
from jax.experimental.pallas import tpu as pltpu
from jax.sharding import PartitionSpec as P

step_size = 0.25
vertical_mix = 0.2
highest = lax.Precision.HIGHEST
f32 = jnp.float32
bf16 = jnp.bfloat16

S = 128
B = 16
R = 8
L = 4
X = 8
Y = 128
GROUP = 16

INV, FWD, FWD_PI = (256 * i for i in range(3))
FWD_Q = 768
COEF_ROWS = 896
EDGE_ROWS = S + 8

vmem = pl.BlockSpec(memory_space=pltpu.VMEM)
hbm = pl.BlockSpec(memory_space=pltpu.HBM)


def row_offsets():
    offsets, at = [], 0
    for group in range(S // GROUP):
        offsets.append(at)
        at += GROUP * (S - GROUP * group)
    return offsets, at


OFFSETS, WEIGHT_ROWS = row_offsets()


def call(kernel, outs, in_specs, name, flops=0, nbytes=1 << 20, scratch=(), place=vmem):
    single = not isinstance(outs, (tuple, list))
    return pl.pallas_call(
        kernel,
        out_shape=outs,
        in_specs=in_specs,
        out_specs=place if single else [place] * len(outs),
        scratch_shapes=list(scratch),
        name=name,
        cost_estimate=pl.CostEstimate(flops=flops, bytes_accessed=nbytes, transcendentals=0),
        compiler_params=pltpu.CompilerParams(vmem_limit_bytes=32 << 20),
    )


def shape(*dims, dtype=f32):
    return jax.ShapeDtypeStruct(dims, dtype)


def swap_groups(tiles):
    group = lax.broadcasted_iota(jnp.int32, (8, Y), 1) // 8
    tiles = list(tiles)
    tiles = [tiles[-i % B] for i in range(B)]
    tiles = [pltpu.roll(tile, 8 * (-i % B), 1) if i else tile for i, tile in enumerate(tiles)]
    for bit in (1, 2, 4, 8):
        upper = (group & bit) != 0
        tiles = [jnp.where(upper, tiles[i - bit], tiles[i]) for i in range(B)]
    return [pltpu.roll(tile, Y - 8 * i, 1) if i else tile for i, tile in enumerate(tiles)]


def run_of(index):
    return jnp.where(lax.axis_index("gy") == 0, index, B - 1 - index)


def own_cells(rows, run):
    shift = lax.rem(Y - 8 * run, Y)
    moved = pltpu.roll(pltpu.roll(rows, shift, 1), 0, 1, stride=8, stride_axis=0)
    group = lax.broadcasted_iota(jnp.int32, (B, Y), 1) // 8
    row = lax.broadcasted_iota(jnp.int32, (B, Y), 0)
    return jnp.sum(jnp.where(group == row, moved, 0.0), axis=0, keepdims=True)


def pack_kernel(
    n_hbm, c_hbm, rate_hbm, vel_hbm, factor_hbm, diff_hbm, kernel_hbm, target_hbm,
    send_ref, own_ref, factor_ref, diff_ref, kernel_ref, target_ref,
    n_ref, c_ref, rate_ref, vel_ref, row_ref, sems,
):
    run = run_of(lax.axis_index("sec"))
    pairs = (
        (factor_hbm, row_ref.at[pl.ds(0, 1)]),
        (diff_hbm, row_ref.at[pl.ds(8, 1)]),
        (rate_hbm, rate_ref),
        (vel_hbm, vel_ref),
        (n_hbm, n_ref),
        (c_hbm, c_ref),
        (kernel_hbm, kernel_ref),
        (target_hbm, target_ref),
    )
    copies = [pltpu.make_async_copy(a, b, sems.at[i]) for i, (a, b) in enumerate(pairs)]
    for copy in copies:
        copy.start()
    for copy in copies[:4]:
        copy.wait()
    rows = [own_cells(rate_ref[pl.ds(h * 16, 16), :], run) for h in range(2)]
    rows += [own_cells(vel_ref[pl.ds(h * 16, 16), :], run) for h in range(4)]
    own_ref[...] = jnp.concatenate(rows + [jnp.zeros((2, Y), f32)], axis=0)
    factor_ref[...] = jnp.broadcast_to(row_ref[pl.ds(0, 1), :], (S, S)).T
    diff_ref[...] = jnp.broadcast_to(row_ref[pl.ds(8, 1), :], (S, S)).T
    for array, ref in enumerate((n_ref, c_ref)):
        copies[4 + array].wait()
        for half in range(2):
            tiles = swap_groups(
                ref[pl.ds(half * 16 + g, R, stride=L * X), :] for g in range(B)
            )
            for d, tile in enumerate(tiles):
                at = pl.multiple_of(run_of(d) * 32 + array * 16 + half * 8, 8)
                send_ref[pl.ds(at, 8), :] = tile
    for copy in copies[6:]:
        copy.wait()


def lane_parts():
    lane = lax.broadcasted_iota(jnp.int32, (8, Y), 1)
    return lane // 64, (lane // 8) % 8, lane % 8


def turn(tile, shift):
    shift = shift % Y
    return tile if shift == 0 else pltpu.roll(tile, shift, 1)


def even_places():
    return lax.rem(lax.axis_index("gx"), 2) == 0, lax.rem(run_of(lax.axis_index("sec")), 2) == 0


def pack_edges(tiles, which, even, refs, rows):
    _, x, y = which
    x_up, x_down, y_up, y_down = (jnp.zeros((8, Y), f32) for _ in range(4))
    for i, tile in enumerate(tiles):
        x_up = jnp.where(x == i, turn(tile, 8 * (i - 7)), x_up)
        x_down = jnp.where(x == 7 - i, turn(tile, 8 * (7 - i)), x_down)
        y_up = jnp.where(y == i, turn(tile, i - 7), y_up)
        y_down = jnp.where(y == 7 - i, turn(tile, 7 - i), y_down)
    for i, (up, down) in enumerate(((x_up, x_down), (y_up, y_down))):
        refs[2 * i][rows, :] = jnp.where(even[i], up, down)
        refs[2 * i + 1][rows, :] = jnp.where(even[i], down, up)


def received_edges(even, refs, rows):
    edges = []
    for i in range(2):
        a, b = (ref[rows, :] for ref in refs[2 * i : 2 * i + 2])
        edges += [jnp.where(even[i], b, a), jnp.where(even[i], a, b)]
    return edges


def shifted(tile, edges, i, which):
    _, x, y = which
    from_low_x, from_high_x, from_low_y, from_high_y = edges
    x_minus = jnp.where(x == 0, turn(from_low_x, -8 * i), turn(tile, 8))
    x_plus = jnp.where(x == 7, turn(from_high_x, 8 * i), turn(tile, -8))
    y_minus = jnp.where(y == 0, turn(from_low_y, -i), turn(tile, 1))
    y_plus = jnp.where(y == 7, turn(from_high_y, i), turn(tile, -1))
    return x_plus, x_minus, y_plus, y_minus


def vertical(low, high, which):
    first = which[0] == 0
    a, b = turn(low, 64), turn(high, 64)
    return (
        a + jnp.where(first, low, b) - 2.0 * low,
        b + jnp.where(first, a, high) - 2.0 * high,
    )


def adjoint_kernel(
    got_ref, own_ref, factor_ref, adj_ref, coef_ref, x_first_ref, x_second_ref, y_first_ref, y_second_ref
):
    block = lax.broadcasted_iota(jnp.int32, (B, Y), 0)
    for h in range(2):
        rate = own_ref[pl.ds(h, 1), :]
        growths, inverses = [], []
        for i in range(R):
            growth = step_size * (rate * factor_ref[pl.ds(i, B, stride=R), :])
            inverse = 1.0 / (1.0 + growth)
            coef_ref[pl.ds(INV + (i * 2 + h) * B, B), :] = inverse
            growths.append(growth)
            inverses.append(inverse)
        product = None
        for i in range(R):
            prior = growths[i - 1] if i else jnp.where(block == 0, 0.0, pltpu.roll(growths[R - 1], 1, 0))
            ratio = prior * inverses[i]
            product = ratio if product is None else ratio * product
            coef_ref[pl.ds(FWD + (i * 2 + h) * B, B), :] = ratio
            coef_ref[pl.ds(FWD_PI + (i * 2 + h) * B, B), :] = product
        q = jnp.where(block == 0, 0.0, product)
        for turns, hop in enumerate((1, 2, 4, 8)):
            coef_ref[pl.ds(FWD_Q + (turns * 2 + h) * B, B), :] = q
            q = q * pltpu.roll(q, hop, 0)
        value, product, values = None, None, []
        for i in reversed(range(R)):
            source = got_ref[pl.ds(16 + h * 8 + i, B, stride=32), :] * inverses[i]
            ratio = growths[i] * inverses[i]
            value = source if value is None else source + ratio * value
            product = ratio if product is None else ratio * product
            values.append((i, value, product))
        q = jnp.where(block == B - 1, 0.0, product)
        for hop in (1, 2, 4, 8):
            value = value + q * pltpu.roll(value, B - hop, 0)
            q = q * pltpu.roll(q, B - hop, 0)
        carry = jnp.where(block == B - 1, 0.0, pltpu.roll(value, B - 1, 0))
        for i, local, product in values:
            adj_ref[pl.ds(h * S + i, B, stride=R), :] = local + product * carry
    which = lane_parts()
    even = even_places()
    refs = (x_first_ref, x_second_ref, y_first_ref, y_second_ref)
    for b in range(B):
        tiles = [got_ref[pl.ds(b * 32 + h * 8, 8), :] for h in range(2)]
        tiles += [adj_ref[pl.ds(h * S + b * 8, 8), :] for h in range(2)]
        pack_edges(tiles, which, even, refs, pl.ds(b * 8, 8))
    winds = [jnp.broadcast_to(own_ref[pl.ds(2 + h, 1), :], (8, Y)) for h in range(4)]
    pack_edges(winds, which, even, refs, pl.ds(S, 8))


def split(value):
    high = value.astype(bf16)
    return high, (value - high.astype(f32)).astype(bf16)


def pair_kernel(
    got_ref, adj_ref, kernel_ref, target_ref, gain_out, coag_out,
    n_ref, a_ref, gain_ref, part_ref, weight_ref, rows_ref,
):
    kernel = kernel_ref[...]
    target = target_ref[...].astype(f32)
    turned = kernel.T
    target_turned = target.T
    same = target == target_turned
    one = 0.5 * kernel + jnp.where(same, 0.5 * turned, 0.0)
    two = jnp.where(same, 0.0, 0.5 * turned)
    for i, part in enumerate((target, target_turned, one, two)):
        rows_ref[pl.ds(i * S, S), :] = part

    for group in range(S // GROUP):
        low = group * GROUP
        count = S - low
        ids = (lax.broadcasted_iota(jnp.int32, (count, S), 0) + low).astype(f32)

        def build(k, _, low=low, count=count, ids=ids, start=OFFSETS[group]):
            t1, t2, one, two = (rows_ref[pl.ds(i * S + low + k, 1), :] for i in range(4))
            high, rest = split(jnp.where(ids == t1, one, jnp.where(ids == t2, two, 0.0)))
            rows = pl.ds(pl.multiple_of(start + k * count, 16), count)
            weight_ref[rows, :] = jnp.concatenate([high, rest], axis=1)
            return 0

        lax.fori_loop(0, GROUP, build, 0, unroll=True)

    for r in range(2):
        for b in range(B):
            n_ref[pl.ds(b * 8, 8), pl.ds(r * Y, Y)] = got_ref[pl.ds(b * 32 + r * 8, 8), :]
        a_ref[:, pl.ds(r * Y, Y)] = adj_ref[pl.ds(r * S, S), :]
    number = n_ref[...]
    high, rest = split(number)
    right = jnp.concatenate([high, high, rest], axis=0)
    gain_ref[...] = jnp.zeros_like(gain_ref)

    for group in range(S // GROUP):
        low = group * GROUP
        count = S - low

        left = weight_ref[pl.ds(OFFSETS[group], GROUP * count), :]
        left = jnp.concatenate([left, left[:, :S]], axis=1)
        found = jnp.dot(left, right, preferred_element_type=f32).reshape(GROUP, count, 2 * Y)
        total = gain_ref[pl.ds(low, count), :]
        adjoint = a_ref[pl.ds(low, count), :]
        for p in range(GROUP):
            k = low + p
            total = total + found[p] * n_ref[pl.ds(k, 1), :]
            share = (found[p] * adjoint).reshape(count // 8, 8, 2 * Y).sum(axis=0)
            for r in range(2):
                part_ref[pl.ds(r * 8 * S + k * 8, 8), :] = share[:, r * Y : (r + 1) * Y]
        gain_ref[pl.ds(low, count), :] = total

    adjoint = a_ref[...]
    pull = jnp.dot(kernel, number, precision=highest, preferred_element_type=f32)
    back = jnp.dot(turned, adjoint * number, precision=highest, preferred_element_type=f32)
    gain = step_size * (0.5 * gain_ref[...] - number * pull)
    for r in range(2):
        gain_out[pl.ds(r * S, S), :] = gain[:, r * Y : (r + 1) * Y]
    other = adjoint * pull + back
    for r in range(2):
        coag = part_ref[pl.ds(r * 8 * S, S, stride=8), :]
        for j in range(1, 8):
            coag = coag + part_ref[pl.ds(r * 8 * S + j, S, stride=8), :]
        coag_out[pl.ds(r * S, S), :] = coag - other[:, r * Y : (r + 1) * Y]


def next_kernel(
    got_ref, adj_ref, own_ref, diff_ref, coef_ref, gain_ref, coag_ref,
    y_second_ref, y_first_ref, x_second_ref, x_first_ref, send_ref, right_ref,
):
    which = lane_parts()
    even = even_places()
    refs = (x_first_ref, x_second_ref, y_first_ref, y_second_ref)
    wind_edges = received_edges(even, refs, pl.ds(S, 8))
    winds = []
    for h in range(2):
        u = jnp.broadcast_to(own_ref[pl.ds(2 + h, 1), :], (8, Y))
        w = jnp.broadcast_to(own_ref[pl.ds(4 + h, 1), :], (8, Y))
        up, um, _, _ = shifted(u, wind_edges, h, which)
        _, _, wp, wm = shifted(w, wind_edges, 2 + h, which)
        winds.append((0.5 * u, 0.5 * w, 0.5 * up, 0.5 * um, 0.5 * wp, 0.5 * wm))
    for b in range(B):
        edges = received_edges(even, refs, pl.ds(b * 8, 8))
        diffusion = diff_ref[pl.ds(b * 8, 8), :]
        numbers = [got_ref[pl.ds(b * 32 + h * 8, 8), :] for h in range(2)]
        adjoints = [adj_ref[pl.ds(h * S + b * 8, 8), :] for h in range(2)]
        number_levels = vertical(*numbers, which)
        adjoint_levels = vertical(*adjoints, which)
        for h in range(2):
            u, w, up, um, wp, wm = winds[h]
            rows = pl.ds(h * S + b * 8, 8)
            v = numbers[h]
            xp, xm, yp, ym = shifted(v, edges, h, which)
            moved = (
                diffusion * (xp + xm + yp + ym - 4.0 * v)
                - u * (xp - xm)
                - w * (yp - ym)
                + vertical_mix * number_levels[h]
            )
            right_ref[rows, :] = v + step_size * moved + gain_ref[rows, :]
            v = adjoints[h]
            xp, xm, yp, ym = shifted(v, edges, 2 + h, which)
            moved = (
                diffusion * (xp + xm + yp + ym - 4.0 * v)
                + (up * xp - um * xm)
                + (wp * yp - wm * ym)
                + vertical_mix * adjoint_levels[h]
            )
            send_ref[pl.ds(b * 32 + 16 + h * 8, 8), :] = v + step_size * (moved + coag_ref[rows, :])
    block = lax.broadcasted_iota(jnp.int32, (B, Y), 0)
    for h in range(2):
        value, values = None, []
        for i in range(R):
            at = (i * 2 + h) * B
            source = right_ref[pl.ds(h * S + i, B, stride=R), :] * coef_ref[pl.ds(INV + at, B), :]
            value = source if value is None else source + coef_ref[pl.ds(FWD + at, B), :] * value
            values.append(value)
        for turns, hop in enumerate((1, 2, 4, 8)):
            q = coef_ref[pl.ds(FWD_Q + (turns * 2 + h) * B, B), :]
            value = value + q * pltpu.roll(value, hop, 0)
        carry = jnp.where(block == 0, 0.0, pltpu.roll(value, 1, 0))
        for i in range(R):
            full = values[i] + coef_ref[pl.ds(FWD_PI + (i * 2 + h) * B, B), :] * carry
            send_ref[pl.ds(h * 8 + i, B, stride=32), :] = full


def unpack_kernel(back_ref, next_hbm, gradient_hbm, next_ref, gradient_ref, sems):
    copies = []
    for array, (ref, out) in enumerate(((next_ref, next_hbm), (gradient_ref, gradient_hbm))):
        for half in range(2):
            tiles = swap_groups(
                back_ref[pl.ds(pl.multiple_of(run_of(d) * 32 + array * 16 + half * 8, 8), 8), :]
                for d in range(B)
            )
            for g, tile in enumerate(tiles):
                ref[pl.ds(half * 16 + g, R, stride=L * X), :] = tile
        copies.append(pltpu.make_async_copy(ref, out, sems.at[array]))
        copies[-1].start()
    for copy in copies:
        copy.wait()


def exchange(rows):
    count = rows.shape[0]
    parts = lax.all_to_all(
        rows.reshape(B, count // B, Y), "sec", split_axis=0, concat_axis=0, tiled=True
    )
    return parts.reshape(count, Y)


def swaps(count, first, place=lambda i: i):
    pairs = [(place(i), place((i + 1) % count)) for i in range(first, count, 2)]
    return pairs + [(b, a) for a, b in pairs]


def y_place(position):
    half, run = position // B, position % B
    return (B - 1 - run if half else run) * 2 + half


def per_device(
    number, cotangent, growth_rate, section_factor, velocity, diffusivity, kernel, target
):
    send, own, factor, diff, kernel_in, target_in = call(
        pack_kernel,
        (
            shape(512, Y), shape(8, Y), shape(S, S), shape(S, S), shape(S, S),
            shape(S, S, dtype=jnp.int32),
        ),
        [hbm] * 8,
        "pack",
        scratch=(
            pltpu.VMEM((256, Y), f32),
            pltpu.VMEM((256, Y), f32),
            pltpu.VMEM((32, Y), f32),
            pltpu.VMEM((64, Y), f32),
            pltpu.VMEM((16, Y), f32),
            pltpu.SemaphoreType.DMA((8,)),
        ),
    )(
        *(
            pltpu.with_memory_space_constraint(array, pltpu.HBM)
            for array in (
                number.reshape(256, Y),
                cotangent.reshape(256, Y),
                growth_rate.reshape(32, Y),
                velocity.reshape(64, Y),
                section_factor.reshape(1, S),
                diffusivity.reshape(1, S),
                kernel,
                target,
            )
        )
    )
    got = exchange(send)
    adj, coef, x_first, x_second, y_first, y_second = call(
        adjoint_kernel,
        (shape(256, Y), shape(COEF_ROWS, Y)) + (shape(EDGE_ROWS, Y),) * 4,
        [vmem] * 3,
        "adjoint",
    )(got, own, factor)
    x_count = lax.axis_size("gx")
    edges = (
        lax.ppermute(x_first, "gx", swaps(x_count, 0)),
        lax.ppermute(x_second, "gx", swaps(x_count, 1)),
        lax.ppermute(y_first, ("sec", "gy"), swaps(2 * B, 0, y_place)),
        lax.ppermute(y_second, ("sec", "gy"), swaps(2 * B, 1, y_place)),
    )
    gain, coag = call(
        pair_kernel,
        (shape(256, Y), shape(256, Y)),
        [vmem] * 4,
        "pairs",
        flops=1 << 32,
        nbytes=8 << 20,
        scratch=(
            pltpu.VMEM((S, 2 * Y), f32),
            pltpu.VMEM((S, 2 * Y), f32),
            pltpu.VMEM((S, 2 * Y), f32),
            pltpu.VMEM((2 * S * 8, Y), f32),
            pltpu.VMEM((WEIGHT_ROWS, 2 * S), bf16),
            pltpu.VMEM((4 * S, S), f32),
        ),
    )(got, adj, kernel_in, target_in)
    send_back = call(
        next_kernel, shape(512, Y), [vmem] * 11, "next", scratch=(pltpu.VMEM((256, Y), f32),)
    )(got, adj, own, diff, coef, gain, coag, *edges[::-1])
    next_rows, gradient = call(
        unpack_kernel,
        (shape(256, Y), shape(256, Y)),
        [vmem],
        "unpack",
        scratch=(
            pltpu.VMEM((256, Y), f32),
            pltpu.VMEM((256, Y), f32),
            pltpu.SemaphoreType.DMA((2,)),
        ),
        place=hbm,
    )(exchange(send_back))
    return next_rows.reshape(number.shape), gradient.reshape(number.shape)


def solution(mesh):
    return jax.shard_map(
        per_device,
        mesh=mesh,
        in_specs=(
            P("sec", None, "gx", "gy"),
            P("sec", None, "gx", "gy"),
            P(None, "gx", "gy"),
            P(),
            P(None, None, "gx", "gy"),
            P(),
            P(),
            P(),
        ),
        out_specs=(P("sec", None, "gx", "gy"), P("sec", None, "gx", "gy")),
        check_vma=False,
    )
```
